32 devices in a mesh: grp: 2 (over y), op: 4 (over z), blk: 2 (over x), rep: 2 (over core).
Axes of the slice: x: 2, y: 2, z: 4, core: 2. Of those that a mesh axis runs over, the one named last changes fastest.
Arguments:
- wavefunction: bfloat16 [96, 128, 128], P(('grp', 'blk', 'rep')), parts along dimension 0, may hold values from -1 to 1
- left_env: bfloat16 [256, 128, 128], P(('grp', 'op')), parts along dimension 0, may hold values from -0.5 to 0.5
- right_env: bfloat16 [256, 128, 128], P(('grp', 'op')), parts along dimension 0, may hold values from -0.5 to 0.5
- slot_table: int32 [3, 4, 2, 2, 2, 64], P(None, 'op', 'blk'), may hold values from 0 to 31, as said below
Outputs:
- sigma_tiles: float32 [128, 96, 128], P(('op', 'rep'), ('grp', 'blk')), parts along dimension 1
The draws below stay inside these ranges and needn't reach their ends.
There are 2 independent parts, one for each index of `grp`. The reference program is written for one: setup_inputs(seed, part) draws one part's arguments, and reference() takes and returns one part's arrays. A program takes and returns all parts, laid end to end along the dimension named above; an argument that names none is the same for every part. Nothing has to cross between parts.
Inputs may be any that keep to these rules, and one draw needn't show every extreme that they name: `slot_table`: at [0, o, b, r, b2, c] a term index below 32 among the terms of op index o; at [1, ...] a target block below 24 of tile group b, or 24 for an empty slot; at [2, ...] a source block below 12 of the wavefunction shard of tile group b2 and sector subset r. Each list of 64 slots has at least one non-empty slot, and in every draw all lists of some op index are full.
All inputs are finite; a program needn't handle non-finite values.
Results may differ from the reference program's by a relative error of at most 0.0029.
Values may be sent and summed in bfloat16 or wider, within the bound.
No kernel may reach another device: no remote copies, remote signals or barrier semaphores. Data moves between devices by JAX's collectives and lax.ppermute only.
A program may use at most 64 MiB of HBM per device.

```python
import jax
import jax.numpy as jnp
from jax import lax

B = 128
NT = 48
TERM_DEV = 32
CAPB = 64
OP_GROUPS = 4
BLK_GROUPS = 2
REP_GROUPS = 2
TERMS = 128
TILES_BLK = 24
TILES_DEV = 12


def draw_slot_table(key, part):
    key = jax.random.fold_in(key, 11)
    subkeys = jax.random.split(key, 7)
    list_count = OP_GROUPS * BLK_GROUPS * REP_GROUPS * BLK_GROUPS
    load_level = jax.random.randint(subkeys[0], (OP_GROUPS,), 1, 9)
    busiest = jax.random.randint(subkeys[1], (), 0, OP_GROUPS)
    load_level = jnp.where(jnp.arange(OP_GROUPS) == busiest, 8, load_level)
    level_list = jnp.repeat(load_level, list_count // OP_GROUPS)
    jitter = jax.random.randint(subkeys[2], (list_count,), 0, CAPB // 8 + 1)
    filled = jnp.maximum(level_list * CAPB // 8 - jnp.where(level_list < 8, jitter, 0), 1)
    scores = jax.random.randint(subkeys[3], (list_count, CAPB), 0, 2 ** 20) * CAPB + jnp.arange(CAPB)[None, :]
    slot_rank = jnp.argsort(jnp.argsort(scores, axis=1), axis=1)
    occupied = slot_rank < filled[:, None]
    term_ids = jax.random.randint(subkeys[4], (list_count, CAPB), 0, TERM_DEV)
    target_ids = jnp.where(occupied, jax.random.randint(subkeys[5], (list_count, CAPB), 0, TILES_BLK), TILES_BLK)
    source_ids = jax.random.randint(subkeys[6], (list_count, CAPB), 0, TILES_DEV)
    stacked = jnp.stack([term_ids, target_ids, source_ids])
    return stacked.reshape(3, OP_GROUPS, BLK_GROUPS, REP_GROUPS, BLK_GROUPS, CAPB).astype(jnp.int32)


def block_scale(rng, shape, shards, low, largest):
    loudness = 1.0
    for position, shards_of in shards:
        steps = jax.random.uniform(jax.random.fold_in(jax.random.fold_in(rng, 6), position), (shards_of,), jnp.float32, low / len(shards), largest / len(shards))
        loudness = loudness * jnp.repeat(jnp.exp(steps), shape[position] // shards_of).reshape((-1,) + (1,) * (len(shape) - 1 - position))
    return loudness


def noise(rng, dims, spread, limit, cuts=(), held_as=jnp.bfloat16):
    level = block_scale(rng, dims, cuts, -0.22, 0.18) if cuts else 1.0
    entries = jax.random.normal(rng, dims, jnp.float32) * spread * level
    return jnp.minimum(jnp.maximum(entries, -limit), limit).astype(held_as)


def setup_inputs(seed: int = 0, part: int = 0) -> dict:
    key_of = jax.random.split(jax.random.key(seed), 5)
    own_keys = jax.random.split(jax.random.fold_in(key_of[4], part), 5)
    wavefunction = noise(own_keys[0], (NT, B, B), (OP_GROUPS * REP_GROUPS * BLK_GROUPS * BLK_GROUPS * CAPB // NT) ** -0.5, 1.0, ((0, 4),))
    left_env = noise(own_keys[1], (TERMS, B, B), B ** -0.5, 0.5, ((0, 4),))
    right_env = noise(own_keys[2], (TERMS, B, B), B ** -0.5, 0.5, ((0, 4),))
    slot_table = draw_slot_table(jax.random.fold_in(key_of[4], 71), part)
    return {"wavefunction": wavefunction, "left_env": left_env, "right_env": right_env, "slot_table": slot_table}


def reference(wavefunction, left_env, right_env, slot_table):
    shape_full = (OP_GROUPS, BLK_GROUPS, REP_GROUPS, BLK_GROUPS, CAPB)
    op_index = lax.broadcasted_iota(jnp.int32, shape_full, 0)
    blk_index = lax.broadcasted_iota(jnp.int32, shape_full, 1)
    rep_index = lax.broadcasted_iota(jnp.int32, shape_full, 2)
    src_blk = lax.broadcasted_iota(jnp.int32, shape_full, 3)
    term_ids = (slot_table[0] + TERM_DEV * op_index).astype(jnp.int32).reshape(-1, CAPB)
    target_ids = jnp.where(slot_table[1] < TILES_BLK, slot_table[1] + TILES_BLK * blk_index, NT).astype(jnp.int32).reshape(-1, CAPB)
    source_ids = (slot_table[2] + TILES_DEV * (src_blk * REP_GROUPS + rep_index)).astype(jnp.int32).reshape(-1, CAPB)

    def one_group(running, slot_group):
        terms_now, targets_now, sources_now = slot_group
        left_rows = left_env[terms_now].astype(jnp.float32)
        tile_rows = wavefunction[sources_now].astype(jnp.float32)
        inner_prod = jnp.einsum("cik,ckj->cij", left_rows, tile_rows).astype(jnp.bfloat16)
        inner_prod = lax.optimization_barrier(inner_prod)
        right_rows = right_env[terms_now].astype(jnp.float32)
        outer_prod = jnp.einsum("cik,cjk->cij", inner_prod.astype(jnp.float32), right_rows)
        return running.at[targets_now].add(outer_prod, mode="drop"), None

    zero_sigma = jnp.zeros((NT, B, B), jnp.float32)
    sigma_sum, _ = lax.scan(one_group, zero_sigma, (term_ids, target_ids, source_ids))
    return jnp.transpose(sigma_sum, (1, 0, 2))
```

```python
import functools

import jax
import jax.numpy as jnp
from jax import lax
from jax.experimental import pallas as pl
from jax.experimental.pallas import tpu as pltpu
from jax.sharding import PartitionSpec as P

VMEM = pl.BlockSpec(memory_space=pltpu.VMEM)
SMEM = pl.BlockSpec(memory_space=pltpu.SMEM)
LINK = jnp.bfloat16


def params():
    return pltpu.CompilerParams(vmem_limit_bytes=24 << 20)


def add_list(table, rep, src, left, right, wave, acc, unroll):
    caps = table.shape[-1]

    def body(step, carry):
        base = step * unroll
        slots = [base + q for q in range(unroll)]
        terms = [table[0, 0, 0, rep, src, c] for c in slots]
        inner = [
            jnp.dot(
                left[terms[q]],
                wave[table[2, 0, 0, rep, src, slots[q]]],
                preferred_element_type=jnp.float32,
            ).astype(jnp.bfloat16)
            for q in range(unroll)
        ]
        outer = [
            lax.dot_general(
                inner[q],
                right[terms[q]],
                (((1,), (1,)), ((), ())),
                preferred_element_type=jnp.float32,
            )
            for q in range(unroll)
        ]
        for q in range(unroll):
            acc[table[1, 0, 0, rep, src, slots[q]]] += outer[q]
        return carry

    lax.fori_loop(0, caps // unroll, body, 0)


def unroll_of(caps):
    return next(u for u in (16, 8, 4, 2, 1) if caps % u == 0)


def own_kernel(where, table, left, right, wave, acc):
    acc[...] = jnp.zeros_like(acc)
    add_list(table, where[0], where[1], left, right, wave, acc, unroll_of(table.shape[-1]))


def other_kernel(where, table, left, right, wave, start, acc):
    acc[...] = start[...]
    add_list(table, where[0], where[1], left, right, wave, acc, unroll_of(table.shape[-1]))


def last_kernel(where, table, left, right, wave, start, keep, send, acc):
    acc[...] = start[...]
    rep = where[0]
    add_list(table, rep, where[1], left, right, wave, acc, unroll_of(table.shape[-1]))
    groups, tiles, rows, _ = keep.shape
    reps = 2
    for g in range(groups):
        mine = pl.multiple_of((g * reps + rep) * rows, rows)
        theirs = pl.multiple_of((g * reps + 1 - rep) * rows, rows)
        keep[g] = acc[pl.ds(0, tiles), pl.ds(mine, rows), :]
        send[g] = acc[pl.ds(0, tiles), pl.ds(theirs, rows), :].astype(LINK)


def pair_kernel(where, keep, got, own, *sends):
    op = where[2]
    own[...] = keep[op] + got[op].astype(jnp.float32)
    for s, out in enumerate(sends):
        to = jnp.bitwise_xor(op, s + 1)
        out[...] = (keep[to] + got[to].astype(jnp.float32)).astype(LINK)


def final_kernel(own, *rest):
    got, out = rest[:-1], rest[-1]
    total = own[...]
    for g in got:
        total = total + g[...].astype(jnp.float32)
    for t in range(total.shape[0]):
        out[:, t, :] = total[t]


def shards(wavefunction, left_env, right_env, slot_table):
    tiles_dev, width, _ = wavefunction.shape
    blk_count = lax.axis_size("blk")
    rep_count = lax.axis_size("rep")
    op_count = lax.axis_size("op")
    tiles_blk = tiles_dev * rep_count
    rep, blk, op = (lax.axis_index(a) for a in ("rep", "blk", "op"))
    row_total = left_env.shape[1]
    rows = row_total // (op_count * rep_count)
    acc_shape = jax.ShapeDtypeStruct((tiles_blk + 1, row_total, width), jnp.float32)

    others = [
        lax.ppermute(wavefunction, "blk", [((i + s) % blk_count, i) for i in range(blk_count)])
        for s in range(1, blk_count)
    ]
    wheres = [
        jnp.stack([rep, (blk + s) % blk_count, op]).astype(jnp.int32) for s in range(blk_count)
    ]
    acc = pl.pallas_call(
        own_kernel,
        out_shape=acc_shape,
        in_specs=[SMEM, SMEM, VMEM, VMEM, VMEM],
        out_specs=VMEM,
        compiler_params=params(),
    )(wheres[0], slot_table, left_env, right_env, wavefunction)

    fast = rep_count == 2 and rows % 16 == 0 and op_count & (op_count - 1) == 0
    middle = others[:-1] if fast else others
    for s, wave in enumerate(middle):
        acc = pl.pallas_call(
            other_kernel,
            out_shape=acc_shape,
            in_specs=[SMEM, SMEM, VMEM, VMEM, VMEM, VMEM],
            out_specs=VMEM,
            compiler_params=params(),
        )(wheres[s + 1], slot_table, left_env, right_env, wave, acc)
    if not fast:
        partial = jnp.swapaxes(acc[:tiles_blk], 0, 1)
        return lax.psum_scatter(partial, ("op", "rep"), scatter_dimension=0, tiled=True)

    part = (op_count, tiles_blk, rows, width)
    keep, send = pl.pallas_call(
        last_kernel,
        out_shape=(
            jax.ShapeDtypeStruct(part, jnp.float32),
            jax.ShapeDtypeStruct(part, LINK),
        ),
        in_specs=[SMEM, SMEM, VMEM, VMEM, VMEM, VMEM],
        out_specs=(VMEM, VMEM),
        scratch_shapes=[pltpu.VMEM(acc_shape.shape, jnp.float32)],
        compiler_params=params(),
    )(wheres[-1], slot_table, left_env, right_env, others[-1], acc)
    got = lax.ppermute(send, "rep", [(0, 1), (1, 0)])
    tile_rows = part[1:]
    own, *sends = pl.pallas_call(
        pair_kernel,
        out_shape=(jax.ShapeDtypeStruct(tile_rows, jnp.float32),)
        + (jax.ShapeDtypeStruct(tile_rows, LINK),) * (op_count - 1),
        in_specs=[SMEM, VMEM, VMEM],
        out_specs=(VMEM,) * op_count,
        compiler_params=params(),
    )(wheres[0], keep, got)
    arrived = [
        lax.ppermute(x, "op", [(i, i ^ (s + 1)) for i in range(op_count)])
        for s, x in enumerate(sends)
    ]
    return pl.pallas_call(
        final_kernel,
        out_shape=jax.ShapeDtypeStruct((rows, tiles_blk, width), jnp.float32),
        in_specs=[VMEM] * op_count,
        out_specs=VMEM,
        compiler_params=params(),
    )(own, *arrived)


def solution(mesh):
    placed = (
        P(("grp", "blk", "rep"), None, None),
        P(("grp", "op"), None, None),
        P(("grp", "op"), None, None),
        P(None, "op", "blk", None, None, None),
    )
    return jax.shard_map(
        shards,
        mesh=mesh,
        in_specs=placed,
        out_specs=P(("op", "rep"), ("grp", "blk"), None),
        check_vma=False,
    )
```

```python
import functools

import jax
import jax.numpy as jnp
from jax import lax
from jax.experimental import pallas as pl
from jax.experimental.pallas import tpu as pltpu
from jax.sharding import PartitionSpec as P

VMEM = pl.BlockSpec(memory_space=pltpu.VMEM)
SMEM = pl.BlockSpec(memory_space=pltpu.SMEM)
ANY = pl.BlockSpec(memory_space=pl.ANY)
LINK = jnp.bfloat16


def params():
    return pltpu.CompilerParams(vmem_limit_bytes=24 << 20)


def add_list(table, rep, src, left, right, wave, acc, unroll):
    caps = table.shape[-1]

    def body(step, carry):
        base = step * unroll
        slots = [base + q for q in range(unroll)]
        terms = [table[0, 0, 0, rep, src, c] for c in slots]
        inner = [
            jnp.dot(
                left[terms[q]],
                wave[table[2, 0, 0, rep, src, slots[q]]],
                preferred_element_type=jnp.float32,
            ).astype(jnp.bfloat16)
            for q in range(unroll)
        ]
        outer = [
            lax.dot_general(
                inner[q],
                right[terms[q]],
                (((1,), (1,)), ((), ())),
                preferred_element_type=jnp.float32,
            )
            for q in range(unroll)
        ]
        for q in range(unroll):
            acc[table[1, 0, 0, rep, src, slots[q]]] += outer[q]
        return carry

    lax.fori_loop(0, caps // unroll, body, 0)


def unroll_of(caps):
    return next(u for u in (16, 8, 4, 2, 1) if caps % u == 0)


def own_kernel(where, table, left, right, wave, acc):
    acc[...] = jnp.zeros_like(acc)
    add_list(table, where[0], where[1], left, right, wave, acc, unroll_of(table.shape[-1]))


def other_kernel(where, table, left, right, wave, start, acc):
    acc[...] = start[...]
    add_list(table, where[0], where[1], left, right, wave, acc, unroll_of(table.shape[-1]))


def last_kernel(where, table, left, right, wave, start, acc, keep_far, keep_near, send_far, send_near):
    rep, op = where[0], where[2]
    add_list(table, rep, where[1], left, right, wave, acc, unroll_of(table.shape[-1]))
    half, tiles, rows, _ = keep_far.shape
    for keep, send, first in ((keep_far, send_far, half), (keep_near, send_near, 0)):
        for g in range(half):
            to = 2 * jnp.bitwise_xor(op, first + g)
            mine = pl.multiple_of((to + rep) * rows, rows)
            theirs = pl.multiple_of((to + 1 - rep) * rows, rows)
            keep[g] = acc[pl.ds(0, tiles), pl.ds(mine, rows), :]
            send[g] = acc[pl.ds(0, tiles), pl.ds(theirs, rows), :].astype(LINK)


def pair_kernel(skip, *refs):
    keep, got = refs[skip : skip + 2]
    for g, out in enumerate(refs[2 * skip + 2 :]):
        out[...] = (keep[g] + got[g].astype(jnp.float32)).astype(out.dtype)


def final_kernel(own, *rest):
    got, out = rest[:-1], rest[-1]
    total = own[...]
    for g in got:
        total = total + g[...].astype(jnp.float32)
    for t in range(total.shape[0]):
        out[:, t, :] = total[t]


def shards(wavefunction, left_env, right_env, slot_table):
    tiles_dev, width, _ = wavefunction.shape
    blk_count = lax.axis_size("blk")
    rep_count = lax.axis_size("rep")
    op_count = lax.axis_size("op")
    tiles_blk = tiles_dev * rep_count
    rep, blk, op = (lax.axis_index(a) for a in ("rep", "blk", "op"))
    row_total = left_env.shape[1]
    rows = row_total // (op_count * rep_count)
    acc_shape = jax.ShapeDtypeStruct((tiles_blk + 1, row_total, width), jnp.float32)

    others = [
        lax.ppermute(wavefunction, "blk", [((i + s) % blk_count, i) for i in range(blk_count)])
        for s in range(1, blk_count)
    ]
    wheres = [
        jnp.stack([rep, (blk + s) % blk_count, op]).astype(jnp.int32) for s in range(blk_count)
    ]
    acc = pl.pallas_call(
        own_kernel,
        out_shape=acc_shape,
        in_specs=[SMEM, SMEM, VMEM, VMEM, VMEM],
        out_specs=VMEM,
        compiler_params=params(),
    )(wheres[0], slot_table, left_env, right_env, wavefunction)

    fast = rep_count == 2 and rows % 16 == 0 and op_count > 1 and op_count & (op_count - 1) == 0
    middle = others[:-1] if fast else others
    for s, wave in enumerate(middle):
        acc = pl.pallas_call(
            other_kernel,
            out_shape=acc_shape,
            in_specs=[SMEM, SMEM, VMEM, VMEM, VMEM, VMEM],
            out_specs=VMEM,
            compiler_params=params(),
        )(wheres[s + 1], slot_table, left_env, right_env, wave, acc)
    if not fast:
        partial = jnp.swapaxes(acc[:tiles_blk], 0, 1)
        return lax.psum_scatter(partial, ("op", "rep"), scatter_dimension=0, tiled=True)

    half = op_count // 2
    part = (half, tiles_blk, rows, width)
    kept = jax.ShapeDtypeStruct(part, jnp.float32)
    sent = jax.ShapeDtypeStruct(part, LINK)
    _, keep_far, keep_near, send_far, send_near = pl.pallas_call(
        last_kernel,
        out_shape=(acc_shape, kept, kept, sent, sent),
        in_specs=[SMEM, SMEM, VMEM, VMEM, VMEM, VMEM],
        out_specs=(VMEM,) * 5,
        input_output_aliases={5: 0},
        compiler_params=params(),
    )(wheres[-1], slot_table, left_env, right_env, others[-1], acc)

    def pair_sum(keep, got, dtypes, later=()):
        out = tuple(jax.ShapeDtypeStruct(part[1:], d) for d in dtypes)
        return pl.pallas_call(
            functools.partial(pair_kernel, len(later)),
            out_shape=tuple(sent for _ in later) + out,
            in_specs=[ANY] * len(later) + [VMEM, VMEM],
            out_specs=(ANY,) * len(later) + (VMEM,) * half,
            input_output_aliases={i: i for i in range(len(later))},
            compiler_params=params(),
        )(*later, keep, got)

    def to_op(x, s):
        return lax.ppermute(x, "op", [(i, i ^ s) for i in range(op_count)])

    got_far = lax.ppermute(send_far, "rep", [(0, 1), (1, 0)])
    send_near, *far = pair_sum(keep_far, got_far, (LINK,) * half, (send_near,))
    arrived = [to_op(x, half + g) for g, x in enumerate(far)]
    got_near = lax.ppermute(send_near, "rep", [(0, 1), (1, 0)])
    own, *near = pair_sum(keep_near, got_near, (jnp.float32,) + (LINK,) * (half - 1))
    arrived = [to_op(x, g + 1) for g, x in enumerate(near)] + arrived
    return pl.pallas_call(
        final_kernel,
        out_shape=jax.ShapeDtypeStruct((rows, tiles_blk, width), jnp.float32),
        in_specs=[VMEM] * op_count,
        out_specs=VMEM,
        compiler_params=params(),
    )(own, *arrived)


def solution(mesh):
    placed = (
        P(("grp", "blk", "rep"), None, None),
        P(("grp", "op"), None, None),
        P(("grp", "op"), None, None),
        P(None, "op", "blk", None, None, None),
    )
    return jax.shard_map(
        shards,
        mesh=mesh,
        in_specs=placed,
        out_specs=P(("op", "rep"), ("grp", "blk"), None),
        check_vma=False,
    )
```

```python
import functools

import jax
import jax.numpy as jnp
from jax import lax
from jax.experimental import pallas as pl
from jax.experimental.pallas import tpu as pltpu
from jax.sharding import PartitionSpec as P

VMEM = pl.BlockSpec(memory_space=pltpu.VMEM)
SMEM = pl.BlockSpec(memory_space=pltpu.SMEM)
ANY = pl.BlockSpec(memory_space=pl.ANY)
LINK = jnp.bfloat16


def params():
    return pltpu.CompilerParams(vmem_limit_bytes=24 << 20)


def in_hbm(x):
    return pltpu.with_memory_space_constraint(x, pltpu.HBM)


def unroll_of(caps, most):
    return next(u for u in (64, 32, 16, 8, 4, 2, 1) if u <= most and caps % u == 0)


def add_list(table, rep, src, left, right_t, wave, acc):
    caps = table.shape[-1]
    unroll = unroll_of(caps, 32)

    def body(step, carry):
        slots = [step * unroll + q for q in range(unroll)]
        terms = [table[0, 0, 0, rep, src, c] for c in slots]
        inner = [
            jnp.dot(
                left[terms[q]],
                wave[table[2, 0, 0, rep, src, slots[q]]],
                preferred_element_type=jnp.float32,
            ).astype(jnp.bfloat16)
            for q in range(unroll)
        ]
        outer = [
            jnp.dot(inner[q], right_t[terms[q]], preferred_element_type=jnp.float32)
            for q in range(unroll)
        ]
        for q in range(unroll):
            acc[table[1, 0, 0, rep, src, slots[q]]] += outer[q]
        return carry

    lax.fori_loop(0, caps // unroll, body, 0)


def prepare_kernel(
    order, left, right, wave, own, other,
    left_rows, right_t, wave_here, own_here, other_here, right_here, sems,
):
    rep, op = lax.axis_index("rep"), lax.axis_index("op")
    rows = left_rows.shape[1] // len(order)
    moves = [(right, right_here), (wave, wave_here), (own, own_here), (other, other_here)]
    for g, s in enumerate(order):
        first = pl.multiple_of((jnp.bitwise_xor(op, s) * 2 + rep) * rows, rows)
        moves.append((left.at[:, pl.ds(first, rows), :], left_rows.at[:, pl.ds(g * rows, rows), :]))
    copies = [pltpu.make_async_copy(a, b, sems.at[i]) for i, (a, b) in enumerate(moves)]
    for copy in copies:
        copy.start()
    for copy in copies:
        copy.wait()
    for k in range(right_t.shape[0]):
        right_t[k] = right_here[k].T


def add_both(table, left_rows, right_t, wave, wave_pair, acc):
    rep, blk = lax.axis_index("rep"), lax.axis_index("blk")
    acc[...] = jnp.zeros_like(acc)
    add_list(table, rep, blk, left_rows, right_t, wave, acc)
    add_list(table, 1 - rep, blk, left_rows, right_t, wave_pair, acc)


def split_rows(acc, outs):
    for g, out in enumerate(outs):
        tiles, rows, _ = out.shape
        out[...] = acc[0:tiles, g * rows : (g + 1) * rows, :].astype(out.dtype)


def other_kernel(table, left_rows, right_t, wave, wave_pair, acc, *outs):
    add_both(table, left_rows, right_t, wave, wave_pair, acc)
    split_rows(acc, outs)


def own_kernel(table, left_rows, right_t, wave, wave_pair, spare, acc, *outs):
    del spare
    add_both(table, left_rows, right_t, wave, wave_pair, acc)
    split_rows(acc, outs)


def sum_kernel(kept, got, out):
    out[...] = (kept[...] + got[...].astype(jnp.float32)).astype(out.dtype)


def final_kernel(own, *rest):
    got, out = rest[:-1], rest[-1]
    total = own[...]
    for g in got:
        total = total + g[...].astype(jnp.float32)
    for t in range(total.shape[0]):
        out[:, t, :] = total[t]


def call(kernel, out_shape, args, ins, outs, **kwargs):
    return pl.pallas_call(
        kernel, out_shape=out_shape, in_specs=ins, out_specs=outs, compiler_params=params(), **kwargs
    )(*args)


def at_source(wavefunction, left_env, right_env, slot_table):
    tiles_dev, width, _ = wavefunction.shape
    terms, row_total, _ = left_env.shape
    op_count = lax.axis_size("op")
    tiles = 2 * tiles_dev
    rows = row_total // (2 * op_count)
    half = op_count // 2
    order = list(range(half, op_count)) + list(range(half - 1, -1, -1))
    swap = [(0, 1), (1, 0)]
    f32, bf16 = jnp.float32, jnp.bfloat16
    shape = jax.ShapeDtypeStruct
    table_spec = pltpu.SMEM(slot_table.shape, slot_table.dtype)
    block = (tiles, rows, width)

    table_other = lax.ppermute(slot_table, "blk", swap)
    wave_pair = lax.ppermute(wavefunction, "rep", swap)
    left_rows, right_t, wave, own_table, other_table = call(
        functools.partial(prepare_kernel, order),
        (
            shape((terms, op_count * rows, width), left_env.dtype),
            shape(right_env.shape, right_env.dtype),
            shape(wavefunction.shape, wavefunction.dtype),
            table_spec,
            table_spec,
        ),
        [in_hbm(x) for x in (left_env, right_env, wavefunction, slot_table)] + [table_other],
        [ANY] * 5,
        (VMEM, VMEM, VMEM, SMEM, SMEM),
        scratch_shapes=[
            pltpu.VMEM(right_env.shape, right_env.dtype),
            pltpu.SemaphoreType.DMA((4 + op_count,)),
        ],
    )
    acc_shape = shape((tiles + 1, op_count * rows, width), f32)
    blocks = [block] * op_count
    acc, *sends = call(
        other_kernel,
        (acc_shape,) + tuple(shape(b, LINK) for b in blocks),
        (other_table, left_rows, right_t, wave, wave_pair),
        [SMEM] + [VMEM] * 4,
        (VMEM,) * (1 + op_count),
    )
    got = [lax.ppermute(x, "blk", swap) for x in sends]
    _, *kept = call(
        own_kernel,
        (acc_shape,) + tuple(shape(b, f32) for b in blocks),
        (own_table, left_rows, right_t, wave, wave_pair, acc),
        [SMEM] + [VMEM] * 5,
        (VMEM,) * (1 + op_count),
        input_output_aliases={5: 0},
    )

    def to_op(x, s):
        return lax.ppermute(x, "op", [(i, i ^ s) for i in range(op_count)])

    arrived = []
    for g in range(op_count - 1):
        total = call(sum_kernel, shape(block, LINK), (kept[g], got[g]), [VMEM] * 2, VMEM)
        arrived.append(to_op(total, order[g]))
    return call(
        final_kernel,
        shape((rows, tiles, width), f32),
        (kept[-1], got[-1], *arrived),
        [VMEM] * (op_count + 1),
        VMEM,
    )


def list_kernel(where, table, left, right, wave, start, acc):
    acc[...] = start[...]
    add_list(table, where[0], where[1], left, right, wave, acc)


def gathered(wavefunction, left_env, right_env, slot_table):
    tiles_dev, width, _ = wavefunction.shape
    blk_count = lax.axis_size("blk")
    tiles_blk = tiles_dev * lax.axis_size("rep")
    rep, blk = lax.axis_index("rep"), lax.axis_index("blk")
    right_t = jnp.swapaxes(right_env, 1, 2)
    acc = jnp.zeros((tiles_blk + 1, left_env.shape[1], width), jnp.float32)
    for s in range(blk_count):
        pairs = [((i + s) % blk_count, i) for i in range(blk_count)]
        acc = call(
            list_kernel,
            jax.ShapeDtypeStruct(acc.shape, acc.dtype),
            (
                jnp.stack([rep, (blk + s) % blk_count]).astype(jnp.int32),
                slot_table,
                left_env,
                right_t,
                lax.ppermute(wavefunction, "blk", pairs) if s else wavefunction,
                acc,
            ),
            [SMEM] * 2 + [VMEM] * 4,
            VMEM,
        )
    partial = jnp.swapaxes(acc[:tiles_blk], 0, 1)
    return lax.psum_scatter(partial, ("op", "rep"), scatter_dimension=0, tiled=True)


def shards(wavefunction, left_env, right_env, slot_table):
    op_count = lax.axis_size("op")
    rows = left_env.shape[1] // (2 * op_count)
    fits = lax.axis_size("rep") == 2 and lax.axis_size("blk") == 2
    fits = fits and op_count > 1 and op_count & (op_count - 1) == 0
    fits = fits and rows % 16 == 0 and rows * 2 * op_count == left_env.shape[1]
    form = at_source if fits else gathered
    return form(wavefunction, left_env, right_env, slot_table)


def solution(mesh):
    placed = (
        P(("grp", "blk", "rep"), None, None),
        P(("grp", "op"), None, None),
        P(("grp", "op"), None, None),
        P(None, "op", "blk", None, None, None),
    )
    return jax.shard_map(
        shards,
        mesh=mesh,
        in_specs=placed,
        out_specs=P(("op", "rep"), ("grp", "blk"), None),
        check_vma=False,
    )
```

```python
import functools

import jax
import jax.numpy as jnp
from jax import lax
from jax.experimental import pallas as pl
from jax.experimental.pallas import tpu as pltpu
from jax.sharding import PartitionSpec as P

VMEM = pl.BlockSpec(memory_space=pltpu.VMEM)
SMEM = pl.BlockSpec(memory_space=pltpu.SMEM)
ANY = pl.BlockSpec(memory_space=pl.ANY)
LINK = jnp.bfloat16


def params():
    return pltpu.CompilerParams(vmem_limit_bytes=24 << 20)


def in_hbm(x):
    return pltpu.with_memory_space_constraint(x, pltpu.HBM)


def unroll_of(caps, most):
    return next(u for u in (64, 32, 16, 8, 4, 2, 1) if u <= most and caps % u == 0)


def add_list(table, rep, src, left, right_t, wave, acc):
    caps = table.shape[-1]
    unroll = unroll_of(caps, 32)

    def body(step, carry):
        slots = [step * unroll + q for q in range(unroll)]
        terms = [table[0, 0, 0, rep, src, c] for c in slots]
        inner = [
            jnp.dot(
                left[terms[q]],
                wave[table[2, 0, 0, rep, src, slots[q]]],
                preferred_element_type=jnp.float32,
            ).astype(jnp.bfloat16)
            for q in range(unroll)
        ]
        outer = [
            jnp.dot(inner[q], right_t[terms[q]], preferred_element_type=jnp.float32)
            for q in range(unroll)
        ]
        for q in range(unroll):
            acc[table[1, 0, 0, rep, src, slots[q]]] += outer[q]
        return carry

    lax.fori_loop(0, caps // unroll, body, 0)


def first_kernel(
    order, left, right, wave, table,
    left_rows, right_t, wave_here, table_here, acc, right_here, sems,
):
    rep, op, blk = lax.axis_index("rep"), lax.axis_index("op"), lax.axis_index("blk")
    rows = left_rows.shape[1] // len(order)
    moves = [(right, right_here), (wave, wave_here), (table, table_here)]
    for g, s in enumerate(order):
        first = pl.multiple_of((jnp.bitwise_xor(op, s) * 2 + rep) * rows, rows)
        moves.append((left.at[:, pl.ds(first, rows), :], left_rows.at[:, pl.ds(g * rows, rows), :]))
    copies = [pltpu.make_async_copy(a, b, sems.at[i]) for i, (a, b) in enumerate(moves)]
    for copy in copies:
        copy.start()
    acc[...] = jnp.zeros_like(acc)
    for copy in copies:
        copy.wait()
    for k in range(right_t.shape[0]):
        right_t[k] = right_here[k].T
    add_list(table_here, rep, blk, left_rows, right_t, wave_here, acc)


def split_rows(acc, outs):
    for g, out in enumerate(outs):
        tiles, rows, _ = out.shape
        out[...] = acc[0:tiles, g * rows : (g + 1) * rows, :].astype(out.dtype)


def own_kernel(table, left_rows, right_t, wave_pair, start, table_other, acc, other_here, *outs):
    del start
    *outs, sem = outs
    rep, blk = lax.axis_index("rep"), lax.axis_index("blk")
    copy = pltpu.make_async_copy(table_other, other_here, sem)
    copy.start()
    add_list(table, 1 - rep, blk, left_rows, right_t, wave_pair, acc)
    split_rows(acc, outs)
    copy.wait()


def other_kernel(table, left_rows, right_t, wave, wave_pair, spare, acc, *outs):
    del spare
    rep, blk = lax.axis_index("rep"), lax.axis_index("blk")
    acc[...] = jnp.zeros_like(acc)
    add_list(table, rep, blk, left_rows, right_t, wave, acc)
    add_list(table, 1 - rep, blk, left_rows, right_t, wave_pair, acc)
    split_rows(acc, outs)


def sum_kernel(kept, got, out):
    out[...] = (kept[...] + got[...].astype(jnp.float32)).astype(out.dtype)


def final_kernel(own, *rest):
    got, out = rest[:-1], rest[-1]
    total = own[...]
    for g in got:
        total = total + g[...].astype(jnp.float32)
    for t in range(total.shape[0]):
        out[:, t, :] = total[t]


def call(kernel, out_shape, args, ins, outs, **kwargs):
    return pl.pallas_call(
        kernel, out_shape=out_shape, in_specs=ins, out_specs=outs, compiler_params=params(), **kwargs
    )(*args)


def at_source(wavefunction, left_env, right_env, slot_table):
    tiles_dev, width, _ = wavefunction.shape
    terms, row_total, _ = left_env.shape
    op_count = lax.axis_size("op")
    tiles = 2 * tiles_dev
    rows = row_total // (2 * op_count)
    half = op_count // 2
    order = list(range(half, op_count)) + list(range(half - 1, -1, -1))
    swap = [(0, 1), (1, 0)]
    f32 = jnp.float32
    shape = jax.ShapeDtypeStruct
    table_spec = pltpu.SMEM(slot_table.shape, slot_table.dtype)
    block = (tiles, rows, width)

    table_other = lax.ppermute(slot_table, "blk", swap)
    wave_pair = lax.ppermute(wavefunction, "rep", swap)
    acc_shape = shape((tiles + 1, op_count * rows, width), f32)
    left_rows, right_t, wave, own_table, acc = call(
        functools.partial(first_kernel, order),
        (
            shape((terms, op_count * rows, width), left_env.dtype),
            shape(right_env.shape, right_env.dtype),
            shape(wavefunction.shape, wavefunction.dtype),
            table_spec,
            acc_shape,
        ),
        [in_hbm(x) for x in (left_env, right_env, wavefunction, slot_table)],
        [ANY] * 4,
        (VMEM, VMEM, VMEM, SMEM, VMEM),
        scratch_shapes=[
            pltpu.VMEM(right_env.shape, right_env.dtype),
            pltpu.SemaphoreType.DMA((3 + op_count,)),
        ],
    )
    acc, other_table, *kept = call(
        own_kernel,
        (acc_shape, table_spec) + (shape(block, f32),) * op_count,
        (own_table, left_rows, right_t, wave_pair, acc, table_other),
        [SMEM] + [VMEM] * 4 + [ANY],
        (VMEM, SMEM) + (VMEM,) * op_count,
        input_output_aliases={4: 0},
        scratch_shapes=[pltpu.SemaphoreType.DMA],
    )
    _, *sends = call(
        other_kernel,
        (acc_shape,) + (shape(block, LINK),) * op_count,
        (other_table, left_rows, right_t, wave, wave_pair, acc),
        [SMEM] + [VMEM] * 5,
        (VMEM,) * (1 + op_count),
        input_output_aliases={5: 0},
    )
    got = [lax.ppermute(x, "blk", swap) for x in sends]

    def to_op(x, s):
        return lax.ppermute(x, "op", [(i, i ^ s) for i in range(op_count)])

    arrived = []
    for g in range(op_count - 1):
        total = call(sum_kernel, shape(block, LINK), (kept[g], got[g]), [VMEM] * 2, VMEM)
        arrived.append(to_op(total, order[g]))
    return call(
        final_kernel,
        shape((rows, tiles, width), f32),
        (kept[-1], got[-1], *arrived),
        [VMEM] * (op_count + 1),
        VMEM,
    )


def list_kernel(where, table, left, right, wave, start, acc):
    acc[...] = start[...]
    add_list(table, where[0], where[1], left, right, wave, acc)


def gathered(wavefunction, left_env, right_env, slot_table):
    tiles_dev, width, _ = wavefunction.shape
    blk_count = lax.axis_size("blk")
    tiles_blk = tiles_dev * lax.axis_size("rep")
    rep, blk = lax.axis_index("rep"), lax.axis_index("blk")
    right_t = jnp.swapaxes(right_env, 1, 2)
    acc = jnp.zeros((tiles_blk + 1, left_env.shape[1], width), jnp.float32)
    for s in range(blk_count):
        pairs = [((i + s) % blk_count, i) for i in range(blk_count)]
        acc = call(
            list_kernel,
            jax.ShapeDtypeStruct(acc.shape, acc.dtype),
            (
                jnp.stack([rep, (blk + s) % blk_count]).astype(jnp.int32),
                slot_table,
                left_env,
                right_t,
                lax.ppermute(wavefunction, "blk", pairs) if s else wavefunction,
                acc,
            ),
            [SMEM] * 2 + [VMEM] * 4,
            VMEM,
        )
    partial = jnp.swapaxes(acc[:tiles_blk], 0, 1)
    return lax.psum_scatter(partial, ("op", "rep"), scatter_dimension=0, tiled=True)


def shards(wavefunction, left_env, right_env, slot_table):
    op_count = lax.axis_size("op")
    rows = left_env.shape[1] // (2 * op_count)
    fits = lax.axis_size("rep") == 2 and lax.axis_size("blk") == 2
    fits = fits and op_count > 1 and op_count & (op_count - 1) == 0
    fits = fits and rows % 16 == 0 and rows * 2 * op_count == left_env.shape[1]
    form = at_source if fits else gathered
    return form(wavefunction, left_env, right_env, slot_table)


def solution(mesh):
    placed = (
        P(("grp", "blk", "rep"), None, None),
        P(("grp", "op"), None, None),
        P(("grp", "op"), None, None),
        P(None, "op", "blk", None, None, None),
    )
    return jax.shard_map(
        shards,
        mesh=mesh,
        in_specs=placed,
        out_specs=P(("op", "rep"), ("grp", "blk"), None),
        check_vma=False,
    )
```

```python
import functools

import jax
import jax.numpy as jnp
from jax import lax
from jax.experimental import pallas as pl
from jax.experimental.pallas import tpu as pltpu
from jax.sharding import PartitionSpec as P

VMEM = pl.BlockSpec(memory_space=pltpu.VMEM)
SMEM = pl.BlockSpec(memory_space=pltpu.SMEM)
ANY = pl.BlockSpec(memory_space=pl.ANY)
LINK = jnp.bfloat16
COSTLY = pl.CostEstimate(flops=16 << 30, bytes_accessed=64 << 20, transcendentals=0)


def params():
    return pltpu.CompilerParams(vmem_limit_bytes=24 << 20)


def in_hbm(x):
    return pltpu.with_memory_space_constraint(x, pltpu.HBM)


def unroll_of(caps, most):
    return next(u for u in (64, 32, 16, 8, 4, 2, 1) if u <= most and caps % u == 0)


def add_list(table, rep, src, left, right_t, wave, acc):
    caps = table.shape[-1]
    unroll = unroll_of(caps, 32)

    def body(step, carry):
        slots = [step * unroll + q for q in range(unroll)]
        terms = [table[0, 0, 0, rep, src, c] for c in slots]
        inner = [
            jnp.dot(
                left[terms[q]],
                wave[table[2, 0, 0, rep, src, slots[q]]],
                preferred_element_type=jnp.float32,
            ).astype(jnp.bfloat16)
            for q in range(unroll)
        ]
        outer = [
            jnp.dot(inner[q], right_t[terms[q]], preferred_element_type=jnp.float32)
            for q in range(unroll)
        ]
        for q in range(unroll):
            acc[table[1, 0, 0, rep, src, slots[q]]] += outer[q]
        return carry

    lax.fori_loop(0, caps // unroll, body, 0)


def first_kernel(
    order, left, right, wave, table,
    left_rows, right_t, wave_here, table_here, acc, right_here, sems,
):
    rep, op, blk = lax.axis_index("rep"), lax.axis_index("op"), lax.axis_index("blk")
    rows = left_rows.shape[1] // len(order)
    moves = [(right, right_here), (wave, wave_here), (table, table_here)]
    for g, s in enumerate(order):
        first = pl.multiple_of((jnp.bitwise_xor(op, s) * 2 + rep) * rows, rows)
        moves.append((left.at[:, pl.ds(first, rows), :], left_rows.at[:, pl.ds(g * rows, rows), :]))
    copies = [pltpu.make_async_copy(a, b, sems.at[i]) for i, (a, b) in enumerate(moves)]
    for copy in copies:
        copy.start()
    acc[...] = jnp.zeros_like(acc)
    for copy in copies:
        copy.wait()
    for k in range(right_t.shape[0]):
        right_t[k] = right_here[k].T
    add_list(table_here, rep, blk, left_rows, right_t, wave_here, acc)


def split_rows(acc, outs):
    first = 0
    for out in outs:
        tiles, rows, _ = out.shape[-3:]
        for g in range(out.shape[0] if len(out.shape) == 4 else 1):
            block = acc[0:tiles, first : first + rows, :].astype(out.dtype)
            if len(out.shape) == 4:
                out[g] = block
            else:
                out[...] = block
            first += rows


def other_kernel(table, left_rows, right_t, wave, wave_pair, *refs):
    *outs, acc, table_here, sem = refs
    rep, blk = lax.axis_index("rep"), lax.axis_index("blk")
    copy = pltpu.make_async_copy(table, table_here, sem)
    copy.start()
    acc[...] = jnp.zeros_like(acc)
    copy.wait()
    add_list(table_here, rep, blk, left_rows, right_t, wave, acc)
    add_list(table_here, 1 - rep, blk, left_rows, right_t, wave_pair, acc)
    split_rows(acc, outs)


def own_kernel(table, left_rows, right_t, wave_pair, start, later, acc, handed_on, *outs):
    del start, later, handed_on
    rep, blk = lax.axis_index("rep"), lax.axis_index("blk")
    add_list(table, 1 - rep, blk, left_rows, right_t, wave_pair, acc)
    split_rows(acc, outs)


def sum_kernel(kept, got, later, out, handed_on):
    del later, handed_on
    out[...] = (kept[...] + got[...].astype(jnp.float32)).astype(out.dtype)


def sums_kernel(kept, got, later, handed_on, *outs):
    del later, handed_on
    for g, out in enumerate(outs):
        out[...] = (kept[g] + got[g].astype(jnp.float32)).astype(out.dtype)


def final_kernel(own, *rest):
    got, out = rest[:-1], rest[-1]
    total = own[...]
    for g in got:
        total = total + g[...].astype(jnp.float32)
    for t in range(total.shape[0]):
        out[:, t, :] = total[t]


def call(kernel, out_shape, args, ins, outs, **kwargs):
    return pl.pallas_call(
        kernel, out_shape=out_shape, in_specs=ins, out_specs=outs, compiler_params=params(), **kwargs
    )(*args)


def at_source(wavefunction, left_env, right_env, slot_table):
    tiles_dev, width, _ = wavefunction.shape
    terms, row_total, _ = left_env.shape
    op_count = lax.axis_size("op")
    tiles = 2 * tiles_dev
    rows = row_total // (2 * op_count)
    half = op_count // 2
    order = list(range(half, op_count)) + list(range(half - 1, -1, -1))
    swap = [(0, 1), (1, 0)]
    f32 = jnp.float32
    shape = jax.ShapeDtypeStruct
    table_spec = pltpu.SMEM(slot_table.shape, slot_table.dtype)
    block = (tiles, rows, width)

    table_other = lax.ppermute(slot_table, "blk", swap)
    wave_pair = lax.ppermute(wavefunction, "rep", swap)
    acc_shape = shape((tiles + 1, op_count * rows, width), f32)
    left_rows, right_t, wave, own_table, acc = call(
        functools.partial(first_kernel, order),
        (
            shape((terms, op_count * rows, width), left_env.dtype),
            shape(right_env.shape, right_env.dtype),
            shape(wavefunction.shape, wavefunction.dtype),
            table_spec,
            acc_shape,
        ),
        [in_hbm(x) for x in (left_env, right_env, wavefunction, slot_table)],
        [ANY] * 4,
        (VMEM, VMEM, VMEM, SMEM, VMEM),
        scratch_shapes=[
            pltpu.VMEM(right_env.shape, right_env.dtype),
            pltpu.SemaphoreType.DMA((3 + op_count,)),
        ],
    )
    blocks = (block, (op_count - 2,) + block, block)
    first, middle, last = call(
        other_kernel,
        tuple(shape(b, LINK) for b in blocks),
        (table_other, left_rows, right_t, wave, wave_pair),
        [ANY] + [VMEM] * 4,
        (VMEM,) * 3,
        scratch_shapes=[
            pltpu.VMEM(acc_shape.shape, f32),
            pltpu.SMEM(slot_table.shape, slot_table.dtype),
            pltpu.SemaphoreType.DMA,
        ],
    )

    def to_blk(x):
        return lax.ppermute(x, "blk", swap)

    def to_op(x, s):
        return lax.ppermute(x, "op", [(i, i ^ s) for i in range(op_count)])

    got_first = to_blk(first)
    _, middle, kept_first, kept_middle, kept_last = call(
        own_kernel,
        (acc_shape, shape(middle.shape, LINK)) + tuple(shape(b, f32) for b in blocks),
        (own_table, left_rows, right_t, wave_pair, acc, middle),
        [SMEM] + [VMEM] * 4 + [ANY],
        (VMEM, ANY) + (VMEM,) * 3,
        input_output_aliases={4: 0, 5: 1},
        cost_estimate=COSTLY,
    )
    got_middle = to_blk(middle)
    total, last = call(
        sum_kernel,
        (shape(block, LINK),) * 2,
        (kept_first, got_first, last),
        [VMEM] * 2 + [ANY],
        (VMEM, ANY),
        input_output_aliases={2: 1},
        cost_estimate=COSTLY,
    )
    arrived = [to_op(total, order[0])]
    last, *totals = call(
        sums_kernel,
        (shape(block, LINK),) * (op_count - 1),
        (kept_middle, got_middle, last),
        [VMEM] * 2 + [ANY],
        (ANY,) + (VMEM,) * (op_count - 2),
        input_output_aliases={2: 0},
    )
    arrived += [to_op(x, s) for x, s in zip(totals, order[1:])]
    return call(
        final_kernel,
        shape((rows, tiles, width), f32),
        (kept_last, to_blk(last), *arrived),
        [VMEM] * (op_count + 1),
        VMEM,
    )


def list_kernel(where, table, left, right, wave, start, acc):
    acc[...] = start[...]
    add_list(table, where[0], where[1], left, right, wave, acc)


def gathered(wavefunction, left_env, right_env, slot_table):
    tiles_dev, width, _ = wavefunction.shape
    blk_count = lax.axis_size("blk")
    tiles_blk = tiles_dev * lax.axis_size("rep")
    rep, blk = lax.axis_index("rep"), lax.axis_index("blk")
    right_t = jnp.swapaxes(right_env, 1, 2)
    acc = jnp.zeros((tiles_blk + 1, left_env.shape[1], width), jnp.float32)
    for s in range(blk_count):
        pairs = [((i + s) % blk_count, i) for i in range(blk_count)]
        acc = call(
            list_kernel,
            jax.ShapeDtypeStruct(acc.shape, acc.dtype),
            (
                jnp.stack([rep, (blk + s) % blk_count]).astype(jnp.int32),
                slot_table,
                left_env,
                right_t,
                lax.ppermute(wavefunction, "blk", pairs) if s else wavefunction,
                acc,
            ),
            [SMEM] * 2 + [VMEM] * 4,
            VMEM,
        )
    partial = jnp.swapaxes(acc[:tiles_blk], 0, 1)
    return lax.psum_scatter(partial, ("op", "rep"), scatter_dimension=0, tiled=True)


def shards(wavefunction, left_env, right_env, slot_table):
    op_count = lax.axis_size("op")
    rows = left_env.shape[1] // (2 * op_count)
    fits = lax.axis_size("rep") == 2 and lax.axis_size("blk") == 2
    fits = fits and op_count > 2 and op_count & (op_count - 1) == 0
    fits = fits and rows % 16 == 0 and rows * 2 * op_count == left_env.shape[1]
    form = at_source if fits else gathered
    return form(wavefunction, left_env, right_env, slot_table)


def solution(mesh):
    placed = (
        P(("grp", "blk", "rep"), None, None),
        P(("grp", "op"), None, None),
        P(("grp", "op"), None, None),
        P(None, "op", "blk", None, None, None),
    )
    return jax.shard_map(
        shards,
        mesh=mesh,
        in_specs=placed,
        out_specs=P(("op", "rep"), ("grp", "blk"), None),
        check_vma=False,
    )
```

```python
import functools

import jax
import jax.numpy as jnp
from jax import lax
from jax.experimental import pallas as pl
from jax.experimental.pallas import tpu as pltpu
from jax.sharding import PartitionSpec as P

VMEM = pl.BlockSpec(memory_space=pltpu.VMEM)
SMEM = pl.BlockSpec(memory_space=pltpu.SMEM)
ANY = pl.BlockSpec(memory_space=pl.ANY)
LINK = jnp.bfloat16
COST_K = None
COST_S = (pl.CostEstimate(flops=int(10.0e9), bytes_accessed=int(10.0e6), transcendentals=0), pl.CostEstimate(flops=int(10.0e9), bytes_accessed=int(10.0e6), transcendentals=0), None)
COST_F = None


def params():
    return pltpu.CompilerParams(vmem_limit_bytes=24 << 20)


def in_hbm(x):
    return pltpu.with_memory_space_constraint(x, pltpu.HBM)


def unroll_of(caps, most):
    return next((u for u in (64, 32, 16, 8, 4, 2, 1) if u <= min(most, caps) and caps % u == 0), 0)


def add_list(table, rep, src, left, right_t, wave, acc, begin=0, end=None):
    end = table.shape[-1] if end is None else end
    unroll = unroll_of(end - begin, 64)

    def body(step, carry):
        slots = [begin + step * unroll + q for q in range(unroll)]
        terms = [table[0, 0, 0, rep, src, c] for c in slots]
        inner = [
            jnp.dot(
                left[terms[q]],
                wave[table[2, 0, 0, rep, src, slots[q]]],
                preferred_element_type=jnp.float32,
            ).astype(jnp.bfloat16)
            for q in range(unroll)
        ]
        outer = [
            jnp.dot(inner[q], right_t[terms[q]], preferred_element_type=jnp.float32)
            for q in range(unroll)
        ]
        for q in range(unroll):
            acc[table[1, 0, 0, rep, src, slots[q]]] += outer[q]
        return carry

    if unroll:
        lax.fori_loop(0, (end - begin) // unroll, body, 0)


def load_kernel(
    order, early, left, right, wave, table, left_rows, right_t, wave_here, table_here, acc, right_here, sems
):
    rep, op = lax.axis_index("rep"), lax.axis_index("op")
    rows = left_rows.shape[1] // len(order)
    moves = [(right, right_here), (wave, wave_here), (table, table_here)]
    for g, s in enumerate(order):
        first = pl.multiple_of((jnp.bitwise_xor(op, s) * 2 + rep) * rows, rows)
        moves.append((left.at[:, pl.ds(first, rows), :], left_rows.at[:, pl.ds(g * rows, rows), :]))
    copies = [pltpu.make_async_copy(a, b, sems.at[i]) for i, (a, b) in enumerate(moves)]
    for copy in copies:
        copy.start()
    acc[...] = jnp.zeros_like(acc)
    for copy in copies:
        copy.wait()
    for k in range(right_t.shape[0]):
        right_t[k] = right_here[k].T
    blk = lax.axis_index("blk")
    add_list(table_here, rep, blk, left_rows, right_t, wave_here, acc, 0, early)


def split_rows(acc, outs):
    first = 0
    for out in outs:
        tiles, rows, _ = out.shape[-3:]
        for to in [out] if len(out.shape) == 3 else [out.at[g] for g in range(out.shape[0])]:
            to[...] = acc[0:tiles, first : first + rows, :].astype(out.dtype)
            first += rows


def other_kernel(
    begin, end, other, table, left_rows, right_t, wave, wave_pair, start, own_acc, *refs
):
    del start
    *outs, acc, other_here, sem = refs
    rep, blk = lax.axis_index("rep"), lax.axis_index("blk")
    copy = pltpu.make_async_copy(other, other_here, sem)
    copy.start()
    acc[...] = jnp.zeros_like(acc)
    add_list(table, rep, blk, left_rows, right_t, wave, own_acc, begin, end)
    copy.wait()
    add_list(other_here, rep, blk, left_rows, right_t, wave, acc)
    add_list(other_here, 1 - rep, blk, left_rows, right_t, wave_pair, acc)
    split_rows(acc, outs)


def own_kernel(begin, table, left_rows, right_t, wave, wave_pair, start, later, acc, handed_on, *outs):
    del start, later, handed_on
    rep, blk = lax.axis_index("rep"), lax.axis_index("blk")
    add_list(table, rep, blk, left_rows, right_t, wave, acc, begin)
    add_list(table, 1 - rep, blk, left_rows, right_t, wave_pair, acc)
    split_rows(acc, outs)


def sum_kernel(kept, got, *refs):
    out = refs[-1]
    out[...] = (kept[...] + got[...].astype(jnp.float32)).astype(out.dtype)


def last_sum_kernel(kept, got, before, *outs):
    del before
    for g, out in enumerate(outs):
        out[...] = (kept[g] + got[g].astype(jnp.float32)).astype(out.dtype)


def final_kernel(own, *rest):
    got, out = rest[:-1], rest[-1]
    total = own[...]
    for g in got:
        total = total + g[...].astype(jnp.float32)
    for t in range(total.shape[0]):
        out[:, t, :] = total[t]


def call(kernel, out_shape, args, ins, outs, **kwargs):
    return pl.pallas_call(
        kernel, out_shape=out_shape, in_specs=ins, out_specs=outs, compiler_params=params(), **kwargs
    )(*args)


def at_source(wavefunction, left_env, right_env, slot_table):
    tiles_dev, width, _ = wavefunction.shape
    terms, row_total, _ = left_env.shape
    op_count = lax.axis_size("op")
    tiles = 2 * tiles_dev
    rows = row_total // (2 * op_count)
    order = [2, 3, 1, 0]
    swap = [(0, 1), (1, 0)]
    f32 = jnp.float32
    shape = jax.ShapeDtypeStruct
    table_spec = pltpu.SMEM(slot_table.shape, slot_table.dtype)
    block = (tiles, rows, width)

    table_other = lax.ppermute(slot_table, "blk", swap)
    wave_pair = lax.ppermute(wavefunction, "rep", swap)
    acc_shape = shape((tiles + 1, op_count * rows, width), f32)
    caps = slot_table.shape[-1]
    early, late = caps // 4, caps // 2
    left_rows, right_t, wave, own_table, acc = call(
        functools.partial(load_kernel, order, early),
        (
            shape((terms, op_count * rows, width), left_env.dtype),
            shape(right_env.shape, right_env.dtype),
            shape(wavefunction.shape, wavefunction.dtype),
            table_spec,
            acc_shape,
        ),
        [in_hbm(x) for x in (left_env, right_env, wavefunction, slot_table)],
        [ANY] * 4,
        (VMEM, VMEM, VMEM, SMEM, VMEM),
        scratch_shapes=[
            pltpu.VMEM(right_env.shape, right_env.dtype),
            pltpu.SemaphoreType.DMA((3 + op_count,)),
        ],
    )
    blocks = (block,) * (op_count - 2) + ((2,) + block,)
    operands = (own_table, left_rows, right_t, wave, wave_pair)
    acc, *sends = call(
        functools.partial(other_kernel, early, late),
        (acc_shape,) + tuple(shape(b, LINK) for b in blocks),
        (table_other, *operands, acc),
        [ANY, SMEM] + [VMEM] * 5,
        (VMEM,) * (1 + len(blocks)),
        input_output_aliases={6: 0},
        scratch_shapes=[
            pltpu.VMEM(acc_shape.shape, f32),
            pltpu.SMEM(slot_table.shape, slot_table.dtype),
            pltpu.SemaphoreType.DMA,
        ],
    )

    def to_blk(x):
        return lax.ppermute(x, "blk", swap)

    def to_op(x, s):
        return lax.ppermute(x, "op", [(i, i ^ s) for i in range(op_count)])

    *far, rest = sends
    got = [to_blk(x) for x in far]
    _, rest, *kept, kept_rest = call(
        functools.partial(own_kernel, late),
        (acc_shape, shape(blocks[-1], LINK)) + tuple(shape(b, f32) for b in blocks),
        (*operands, acc, rest),
        [SMEM] + [VMEM] * 5 + [ANY],
        (VMEM, ANY) + (VMEM,) * len(blocks),
        input_output_aliases={5: 0, 6: 1},
        cost_estimate=COST_K,
    )
    got_rest = to_blk(rest)
    arrived, before = [], ()
    for g, s in enumerate(order[:-2]):
        total = call(
            sum_kernel,
            shape(block, LINK),
            (kept[g], got[g], *before),
            [VMEM] * 2 + [ANY] * len(before),
            VMEM,
            cost_estimate=COST_S[g],
        )
        arrived.append(to_op(total, s))
        before = (total,)
    near, own = call(
        last_sum_kernel,
        (shape(block, LINK), shape(block, f32)),
        (kept_rest, got_rest, *before),
        [VMEM] * 2 + [ANY],
        (VMEM,) * 2,
        cost_estimate=COST_S[2],
    )
    arrived.append(to_op(near, order[-2]))
    return call(
        final_kernel,
        shape((rows, tiles, width), f32),
        (own, *arrived),
        [VMEM] * op_count,
        VMEM,
        cost_estimate=COST_F,
    )


def list_kernel(where, table, left, right, wave, start, acc):
    acc[...] = start[...]
    add_list(table, where[0], where[1], left, right, wave, acc)


def gathered(wavefunction, left_env, right_env, slot_table):
    tiles_dev, width, _ = wavefunction.shape
    blk_count = lax.axis_size("blk")
    tiles_blk = tiles_dev * lax.axis_size("rep")
    rep, blk = lax.axis_index("rep"), lax.axis_index("blk")
    right_t = jnp.swapaxes(right_env, 1, 2)
    acc = jnp.zeros((tiles_blk + 1, left_env.shape[1], width), jnp.float32)
    for s in range(blk_count):
        pairs = [((i + s) % blk_count, i) for i in range(blk_count)]
        acc = call(
            list_kernel,
            jax.ShapeDtypeStruct(acc.shape, acc.dtype),
            (
                jnp.stack([rep, (blk + s) % blk_count]).astype(jnp.int32),
                slot_table,
                left_env,
                right_t,
                lax.ppermute(wavefunction, "blk", pairs) if s else wavefunction,
                acc,
            ),
            [SMEM] * 2 + [VMEM] * 4,
            VMEM,
        )
    partial = jnp.swapaxes(acc[:tiles_blk], 0, 1)
    return lax.psum_scatter(partial, ("op", "rep"), scatter_dimension=0, tiled=True)


def shards(wavefunction, left_env, right_env, slot_table):
    op_count = lax.axis_size("op")
    rows = left_env.shape[1] // (2 * op_count)
    fits = lax.axis_size("rep") == 2 and lax.axis_size("blk") == 2
    fits = fits and op_count > 2 and op_count & (op_count - 1) == 0
    fits = fits and rows % 16 == 0 and rows * 2 * op_count == left_env.shape[1]
    form = at_source if fits else gathered
    return form(wavefunction, left_env, right_env, slot_table)


def solution(mesh):
    placed = (
        P(("grp", "blk", "rep"), None, None),
        P(("grp", "op"), None, None),
        P(("grp", "op"), None, None),
        P(None, "op", "blk", None, None, None),
    )
    return jax.shard_map(
        shards,
        mesh=mesh,
        in_specs=placed,
        out_specs=P(("op", "rep"), ("grp", "blk"), None),
        check_vma=False,
    )
```

```python
import functools

import jax
import jax.numpy as jnp
from jax import lax
from jax.experimental import pallas as pl
from jax.experimental.pallas import tpu as pltpu
from jax.sharding import PartitionSpec as P

VMEM = pl.BlockSpec(memory_space=pltpu.VMEM)
SMEM = pl.BlockSpec(memory_space=pltpu.SMEM)
ANY = pl.BlockSpec(memory_space=pl.ANY)
LINK = jnp.bfloat16
COSTLY = pl.CostEstimate(flops=10**10, bytes_accessed=10**7, transcendentals=0)


def params():
    return pltpu.CompilerParams(vmem_limit_bytes=24 << 20)


def in_hbm(x):
    return pltpu.with_memory_space_constraint(x, pltpu.HBM)


def unroll_of(caps, most):
    return next((u for u in range(min(most, caps), 0, -1) if caps % u == 0), 0)


def add_list(table, rep, src, left, right_t, wave, acc, begin=0, end=None):
    end = table.shape[-1] if end is None else end
    unroll = unroll_of(end - begin, 64)

    def body(step, carry):
        slots = [begin + step * unroll + q for q in range(unroll)]
        terms = [table[0, 0, 0, rep, src, c] for c in slots]
        inner = [
            jnp.dot(
                left[terms[q]],
                wave[table[2, 0, 0, rep, src, slots[q]]],
                preferred_element_type=jnp.float32,
            ).astype(jnp.bfloat16)
            for q in range(unroll)
        ]
        outer = [
            jnp.dot(inner[q], right_t[terms[q]], preferred_element_type=jnp.float32)
            for q in range(unroll)
        ]
        for q in range(unroll):
            acc[table[1, 0, 0, rep, src, slots[q]]] += outer[q]
        return carry

    if unroll:
        lax.fori_loop(0, (end - begin) // unroll, body, 0)


def load_kernel(
    order, left, right, wave, table,
    left_rows, right_t, wave_here, table_here, acc, right_here, sems,
):
    rep, op = lax.axis_index("rep"), lax.axis_index("op")
    rows = left_rows.shape[1] // len(order)
    count = right_t.shape[0]
    part = next(p for p in (8, 4, 2, 1) if count % p == 0)
    moves = [(table, table_here)]
    for k in range(0, count, part):
        moves.append((right.at[pl.ds(k, part)], right_here.at[pl.ds(k, part)]))
    for g, s in enumerate(order):
        first = pl.multiple_of((jnp.bitwise_xor(op, s) * 2 + rep) * rows, rows)
        moves.append((left.at[:, pl.ds(first, rows), :], left_rows.at[:, pl.ds(g * rows, rows), :]))
    moves.append((wave, wave_here))
    copies = [pltpu.make_async_copy(a, b, sems.at[i]) for i, (a, b) in enumerate(moves)]
    for copy in copies:
        copy.start()
    acc[...] = jnp.zeros_like(acc)
    copies[0].wait()
    for k in range(count):
        if k % part == 0:
            copies[1 + k // part].wait()
        right_t[k] = right_here[k].T
    for copy in copies[1 + count // part :]:
        copy.wait()


def split_rows(acc, outs):
    first = 0
    for out in outs:
        tiles, rows, _ = out.shape[-3:]
        for to in [out] if len(out.shape) == 3 else [out.at[g] for g in range(out.shape[0])]:
            to[...] = acc[0:tiles, first : first + rows, :].astype(out.dtype)
            first += rows


def other_kernel(
    early, other, table, left_rows, right_t, wave, start, own_acc, other_here, acc, sem
):
    del start
    rep, blk = lax.axis_index("rep"), lax.axis_index("blk")
    copy = pltpu.make_async_copy(other, other_here, sem)
    copy.start()
    acc[...] = jnp.zeros_like(acc)
    add_list(table, rep, blk, left_rows, right_t, wave, own_acc, 0, early)
    copy.wait()
    add_list(other_here, rep, blk, left_rows, right_t, wave, acc)


def pair_kernel(table, left_rows, right_t, wave_pair, start, acc, *outs):
    del start
    rep, blk = lax.axis_index("rep"), lax.axis_index("blk")
    add_list(table, 1 - rep, blk, left_rows, right_t, wave_pair, acc)
    split_rows(acc, outs)


def own_kernel(early, table, left_rows, right_t, wave, wave_pair, start, acc):
    del start
    rep, blk = lax.axis_index("rep"), lax.axis_index("blk")
    add_list(table, rep, blk, left_rows, right_t, wave, acc, early)
    add_list(table, 1 - rep, blk, left_rows, right_t, wave_pair, acc)


def add_block(acc, block, got, out):
    tiles, rows, _ = out.shape
    kept = acc[0:tiles, block * rows : (block + 1) * rows, :]
    out[...] = (kept + got[...].astype(jnp.float32)).astype(out.dtype)


def sum_kernel(block, acc, got, *refs):
    add_block(acc, block, got, refs[-1])


def last_sum_kernel(first, acc, got, before, *outs):
    del before
    for g, out in enumerate(outs):
        add_block(acc, first + g, got.at[g], out)


def final_kernel(own, *rest):
    got, out = rest[:-1], rest[-1]
    total = own[...]
    for g in got:
        total = total + g[...].astype(jnp.float32)
    for t in range(total.shape[0]):
        out[:, t, :] = total[t]


def call(kernel, out_shape, args, ins, outs, **kwargs):
    return pl.pallas_call(
        kernel, out_shape=out_shape, in_specs=ins, out_specs=outs, compiler_params=params(), **kwargs
    )(*args)


def at_source(wavefunction, left_env, right_env, slot_table):
    tiles_dev, width, _ = wavefunction.shape
    terms, row_total, _ = left_env.shape
    op_count = lax.axis_size("op")
    tiles = 2 * tiles_dev
    rows = row_total // (2 * op_count)
    order = [*range(op_count // 2, op_count), *range(op_count // 2 - 1, -1, -1)]
    swap = [(0, 1), (1, 0)]
    f32 = jnp.float32
    shape = jax.ShapeDtypeStruct
    table_spec = pltpu.SMEM(slot_table.shape, slot_table.dtype)
    block = (tiles, rows, width)

    across = [(0, 3), (1, 2), (2, 1), (3, 0)]
    table_other = lax.ppermute(slot_table, ("blk", "rep"), across)
    wave_pair = lax.ppermute(wavefunction, "rep", swap)
    acc_shape = shape((tiles + 1, op_count * rows, width), f32)
    caps = slot_table.shape[-1]
    early = caps // 8
    left_shape = shape((terms, op_count * rows, width), left_env.dtype)
    left_rows, right_t, wave, own_table, acc = call(
        functools.partial(load_kernel, order),
        (
            left_shape,
            shape(right_env.shape, right_env.dtype),
            shape(wavefunction.shape, wavefunction.dtype),
            table_spec,
            acc_shape,
        ),
        [in_hbm(x) for x in (left_env, right_env, wavefunction, slot_table)],
        [ANY] * 4,
        (VMEM, VMEM, VMEM, SMEM, VMEM),
        scratch_shapes=[
            pltpu.VMEM(right_env.shape, right_env.dtype),
            pltpu.SemaphoreType.DMA((2 + op_count + terms,)),
        ],
    )
    blocks = (block,) * (op_count - 2) + ((2,) + block,)
    acc, other_table, acc_other = call(
        functools.partial(other_kernel, early),
        (acc_shape, table_spec, acc_shape),
        (table_other, own_table, left_rows, right_t, wave, acc),
        [ANY, SMEM] + [VMEM] * 4,
        (VMEM, SMEM, VMEM),
        input_output_aliases={5: 0},
        scratch_shapes=[pltpu.SemaphoreType.DMA],
        cost_estimate=COSTLY,
    )
    _, *sends = call(
        pair_kernel,
        (acc_shape,) + tuple(shape(b, LINK) for b in blocks),
        (other_table, left_rows, right_t, wave_pair, acc_other),
        [SMEM] + [VMEM] * 4,
        (VMEM,) * (1 + len(blocks)),
        input_output_aliases={4: 0},
    )

    def to_blk(x):
        return lax.ppermute(x, "blk", swap)

    def to_op(x, s):
        return lax.ppermute(x, "op", [(i, i ^ s) for i in range(op_count)])

    *far, rest = sends
    got = [to_blk(x) for x in far]
    acc = call(
        functools.partial(own_kernel, early),
        acc_shape,
        (own_table, left_rows, right_t, wave, wave_pair, acc),
        [SMEM] + [VMEM] * 5,
        VMEM,
        input_output_aliases={5: 0},
    )
    got_rest = to_blk(rest)
    arrived, before = [], ()
    for g, s in enumerate(order[:-2]):
        total = call(
            functools.partial(sum_kernel, g),
            shape(block, LINK),
            (acc, got[g], *before),
            [VMEM] * 2 + [ANY] * len(before),
            VMEM,
            cost_estimate=COSTLY,
        )
        arrived.append(to_op(total, s))
        before = (total,)
    near, own = call(
        functools.partial(last_sum_kernel, op_count - 2),
        (shape(block, LINK), shape(block, f32)),
        (acc, got_rest, *before),
        [VMEM] * 2 + [ANY],
        (VMEM,) * 2,
    )
    arrived.append(to_op(near, order[-2]))
    return call(
        final_kernel,
        shape((rows, tiles, width), f32),
        (own, *arrived),
        [VMEM] * op_count,
        VMEM,
    )


def list_kernel(where, table, left, right, wave, start, acc):
    acc[...] = start[...]
    add_list(table, where[0], where[1], left, right, wave, acc)


def gathered(wavefunction, left_env, right_env, slot_table):
    tiles_dev, width, _ = wavefunction.shape
    blk_count = lax.axis_size("blk")
    tiles_blk = tiles_dev * lax.axis_size("rep")
    rep, blk = lax.axis_index("rep"), lax.axis_index("blk")
    right_t = jnp.swapaxes(right_env, 1, 2)
    acc = jnp.zeros((tiles_blk + 1, left_env.shape[1], width), jnp.float32)
    for s in range(blk_count):
        pairs = [((i + s) % blk_count, i) for i in range(blk_count)]
        acc = call(
            list_kernel,
            jax.ShapeDtypeStruct(acc.shape, acc.dtype),
            (
                jnp.stack([rep, (blk + s) % blk_count]).astype(jnp.int32),
                slot_table,
                left_env,
                right_t,
                lax.ppermute(wavefunction, "blk", pairs) if s else wavefunction,
                acc,
            ),
            [SMEM] * 2 + [VMEM] * 4,
            VMEM,
        )
    partial = jnp.swapaxes(acc[:tiles_blk], 0, 1)
    return lax.psum_scatter(partial, ("op", "rep"), scatter_dimension=0, tiled=True)


def shards(wavefunction, left_env, right_env, slot_table):
    op_count = lax.axis_size("op")
    rows = left_env.shape[1] // (2 * op_count)
    fits = lax.axis_size("rep") == 2 and lax.axis_size("blk") == 2
    fits = fits and op_count > 2 and op_count & (op_count - 1) == 0
    fits = fits and rows % 16 == 0 and rows * 2 * op_count == left_env.shape[1]
    form = at_source if fits else gathered
    return form(wavefunction, left_env, right_env, slot_table)


def solution(mesh):
    placed = (
        P(("grp", "blk", "rep"), None, None),
        P(("grp", "op"), None, None),
        P(("grp", "op"), None, None),
        P(None, "op", "blk", None, None, None),
    )
    return jax.shard_map(
        shards,
        mesh=mesh,
        in_specs=placed,
        out_specs=P(("op", "rep"), ("grp", "blk"), None),
        check_vma=False,
    )
```

```python
import functools

import jax
import jax.numpy as jnp
from jax import lax
from jax.experimental import pallas as pl
from jax.experimental.pallas import tpu as pltpu
from jax.sharding import PartitionSpec as P

VMEM = pl.BlockSpec(memory_space=pltpu.VMEM)
SMEM = pl.BlockSpec(memory_space=pltpu.SMEM)
ANY = pl.BlockSpec(memory_space=pl.ANY)
LINK = jnp.bfloat16
COSTLY = pl.CostEstimate(flops=10**10, bytes_accessed=10**7, transcendentals=0)


def params():
    return pltpu.CompilerParams(vmem_limit_bytes=24 << 20)


def in_hbm(x):
    return pltpu.with_memory_space_constraint(x, pltpu.HBM)


def unroll_of(caps, most):
    return next((u for u in range(min(most, caps), 0, -1) if caps % u == 0), 0)


def add_list(table, rep, src, left, right_t, wave, acc, begin=0, end=None):
    end = table.shape[-1] if end is None else end
    unroll = unroll_of(end - begin, 64)

    def body(step, carry):
        slots = [begin + step * unroll + q for q in range(unroll)]
        terms = [table[0, 0, 0, rep, src, c] for c in slots]
        inner = [
            jnp.dot(
                left[terms[q]],
                wave[table[2, 0, 0, rep, src, slots[q]]],
                preferred_element_type=jnp.float32,
            ).astype(jnp.bfloat16)
            for q in range(unroll)
        ]
        outer = [
            jnp.dot(inner[q], right_t[terms[q]], preferred_element_type=jnp.float32)
            for q in range(unroll)
        ]
        for q in range(unroll):
            acc[table[1, 0, 0, rep, src, slots[q]]] += outer[q]
        return carry

    if unroll:
        lax.fori_loop(0, (end - begin) // unroll, body, 0)


def load_kernel(
    order, left, right, wave, table,
    left_rows, right_t, wave_here, table_here, right_here, sems,
):
    rep, op = lax.axis_index("rep"), lax.axis_index("op")
    rows = left_rows.shape[1] // len(order)
    count = right_t.shape[0]
    part = next(p for p in (8, 4, 2, 1) if count % p == 0)
    moves = [(table, table_here)]
    for k in range(0, count, part):
        moves.append((right.at[pl.ds(k, part)], right_here.at[pl.ds(k, part)]))
    for g, s in enumerate(order):
        first = pl.multiple_of((jnp.bitwise_xor(op, s) * 2 + rep) * rows, rows)
        moves.append((left.at[:, pl.ds(first, rows), :], left_rows.at[:, pl.ds(g * rows, rows), :]))
    moves.append((wave, wave_here))
    copies = [pltpu.make_async_copy(a, b, sems.at[i]) for i, (a, b) in enumerate(moves)]
    for copy in copies:
        copy.start()
    copies[0].wait()
    for k in range(count):
        if k % part == 0:
            copies[1 + k // part].wait()
        right_t[k] = right_here[k].T
    for copy in copies[1 + count // part :]:
        copy.wait()


def split_rows(acc, outs):
    first = 0
    for out in outs:
        tiles, rows, _ = out.shape[-3:]
        for to in [out] if len(out.shape) == 3 else [out.at[g] for g in range(out.shape[0])]:
            to[...] = acc[0:tiles, first : first + rows, :].astype(out.dtype)
            first += rows


def other_kernel(
    early, other, table, left_rows, right_t, wave, own_acc, other_here, acc, sem
):
    rep, blk = lax.axis_index("rep"), lax.axis_index("blk")
    copy = pltpu.make_async_copy(other, other_here, sem)
    copy.start()
    own_acc[...] = jnp.zeros_like(own_acc)
    acc[...] = jnp.zeros_like(acc)
    add_list(table, rep, blk, left_rows, right_t, wave, own_acc, 0, early)
    copy.wait()
    add_list(other_here, rep, blk, left_rows, right_t, wave, acc)


def pair_kernel(table, left_rows, right_t, wave_pair, start, *refs):
    *outs, acc = refs
    acc[...] = start[...]
    rep, blk = lax.axis_index("rep"), lax.axis_index("blk")
    add_list(table, 1 - rep, blk, left_rows, right_t, wave_pair, acc)
    split_rows(acc, outs)


def own_kernel(early, table, left_rows, right_t, wave, wave_pair, start, acc):
    acc[...] = start[...]
    rep, blk = lax.axis_index("rep"), lax.axis_index("blk")
    add_list(table, rep, blk, left_rows, right_t, wave, acc, early)
    add_list(table, 1 - rep, blk, left_rows, right_t, wave_pair, acc)


def add_block(acc, block, got, out):
    tiles, rows, _ = out.shape
    kept = acc[0:tiles, block * rows : (block + 1) * rows, :]
    out[...] = (kept + got[...].astype(jnp.float32)).astype(out.dtype)


def sum_kernel(block, acc, got, *refs):
    add_block(acc, block, got, refs[-1])


def last_sum_kernel(first, acc, got, before, *outs):
    del before
    for g, out in enumerate(outs):
        add_block(acc, first + g, got.at[g], out)


def final_kernel(own, *rest):
    got, out = rest[:-1], rest[-1]
    total = own[...]
    for g in got:
        total = total + g[...].astype(jnp.float32)
    for t in range(total.shape[0]):
        out[:, t, :] = total[t]


def call(kernel, out_shape, args, ins, outs, **kwargs):
    return pl.pallas_call(
        kernel, out_shape=out_shape, in_specs=ins, out_specs=outs, compiler_params=params(), **kwargs
    )(*args)


def at_source(wavefunction, left_env, right_env, slot_table):
    tiles_dev, width, _ = wavefunction.shape
    terms, row_total, _ = left_env.shape
    op_count = lax.axis_size("op")
    tiles = 2 * tiles_dev
    rows = row_total // (2 * op_count)
    order = [*range(op_count // 2, op_count), *range(op_count // 2 - 1, -1, -1)]
    swap = [(0, 1), (1, 0)]
    f32 = jnp.float32
    shape = jax.ShapeDtypeStruct
    table_spec = pltpu.SMEM(slot_table.shape, slot_table.dtype)
    block = (tiles, rows, width)

    across = [(0, 3), (1, 2), (2, 1), (3, 0)]
    table_other = lax.ppermute(slot_table, ("blk", "rep"), across)
    wave_pair = lax.ppermute(wavefunction, "rep", swap)
    acc_shape = shape((tiles + 1, op_count * rows, width), f32)
    caps = slot_table.shape[-1]
    early = caps // 8
    left_shape = shape((terms, op_count * rows, width), left_env.dtype)
    left_rows, right_t, wave, own_table = call(
        functools.partial(load_kernel, order),
        (
            left_shape,
            shape(right_env.shape, right_env.dtype),
            shape(wavefunction.shape, wavefunction.dtype),
            table_spec,
        ),
        [in_hbm(x) for x in (left_env, right_env, wavefunction, slot_table)],
        [ANY] * 4,
        (VMEM, VMEM, VMEM, SMEM),
        scratch_shapes=[
            pltpu.VMEM(right_env.shape, right_env.dtype),
            pltpu.SemaphoreType.DMA((2 + op_count + terms,)),
        ],
    )
    blocks = (block,) * (op_count - 2) + ((2,) + block,)
    acc, other_table, acc_other = call(
        functools.partial(other_kernel, early),
        (acc_shape, table_spec, acc_shape),
        (table_other, own_table, left_rows, right_t, wave),
        [ANY, SMEM] + [VMEM] * 3,
        (VMEM, SMEM, VMEM),
        scratch_shapes=[pltpu.SemaphoreType.DMA],
        cost_estimate=COSTLY,
    )
    sends = call(
        pair_kernel,
        tuple(shape(b, LINK) for b in blocks),
        (other_table, left_rows, right_t, wave_pair, acc_other),
        [SMEM] + [VMEM] * 4,
        (VMEM,) * len(blocks),
        scratch_shapes=[pltpu.VMEM(acc_shape.shape, f32)],
    )

    def to_blk(x):
        return lax.ppermute(x, "blk", swap)

    def to_op(x, s):
        return lax.ppermute(x, "op", [(i, i ^ s) for i in range(op_count)])

    *far, rest = sends
    got = [to_blk(x) for x in far]
    acc = call(
        functools.partial(own_kernel, early),
        acc_shape,
        (own_table, left_rows, right_t, wave, wave_pair, acc),
        [SMEM] + [VMEM] * 5,
        VMEM,
    )
    got_rest = to_blk(rest)
    arrived, before = [], ()
    for g, s in enumerate(order[:-2]):
        total = call(
            functools.partial(sum_kernel, g),
            shape(block, LINK),
            (acc, got[g], *before),
            [VMEM] * 2 + [ANY] * len(before),
            VMEM,
            cost_estimate=COSTLY,
        )
        arrived.append(to_op(total, s))
        before = (total,)
    near, own = call(
        functools.partial(last_sum_kernel, op_count - 2),
        (shape(block, LINK), shape(block, f32)),
        (acc, got_rest, *before),
        [VMEM] * 2 + [ANY],
        (VMEM,) * 2,
    )
    arrived.append(to_op(near, order[-2]))
    return call(
        final_kernel,
        shape((rows, tiles, width), f32),
        (own, *arrived),
        [VMEM] * op_count,
        VMEM,
    )


def list_kernel(where, table, left, right, wave, start, acc):
    acc[...] = start[...]
    add_list(table, where[0], where[1], left, right, wave, acc)


def gathered(wavefunction, left_env, right_env, slot_table):
    tiles_dev, width, _ = wavefunction.shape
    blk_count = lax.axis_size("blk")
    tiles_blk = tiles_dev * lax.axis_size("rep")
    rep, blk = lax.axis_index("rep"), lax.axis_index("blk")
    right_t = jnp.swapaxes(right_env, 1, 2)
    acc = jnp.zeros((tiles_blk + 1, left_env.shape[1], width), jnp.float32)
    for s in range(blk_count):
        pairs = [((i + s) % blk_count, i) for i in range(blk_count)]
        acc = call(
            list_kernel,
            jax.ShapeDtypeStruct(acc.shape, acc.dtype),
            (
                jnp.stack([rep, (blk + s) % blk_count]).astype(jnp.int32),
                slot_table,
                left_env,
                right_t,
                lax.ppermute(wavefunction, "blk", pairs) if s else wavefunction,
                acc,
            ),
            [SMEM] * 2 + [VMEM] * 4,
            VMEM,
        )
    partial = jnp.swapaxes(acc[:tiles_blk], 0, 1)
    return lax.psum_scatter(partial, ("op", "rep"), scatter_dimension=0, tiled=True)


def shards(wavefunction, left_env, right_env, slot_table):
    op_count = lax.axis_size("op")
    rows = left_env.shape[1] // (2 * op_count)
    fits = lax.axis_size("rep") == 2 and lax.axis_size("blk") == 2
    fits = fits and op_count > 2 and op_count & (op_count - 1) == 0
    fits = fits and rows % 16 == 0 and rows * 2 * op_count == left_env.shape[1]
    form = at_source if fits else gathered
    return form(wavefunction, left_env, right_env, slot_table)


def solution(mesh):
    placed = (
        P(("grp", "blk", "rep"), None, None),
        P(("grp", "op"), None, None),
        P(("grp", "op"), None, None),
        P(None, "op", "blk", None, None, None),
    )
    return jax.shard_map(
        shards,
        mesh=mesh,
        in_specs=placed,
        out_specs=P(("op", "rep"), ("grp", "blk"), None),
        check_vma=False,
    )
```

```python
import functools

import jax
import jax.numpy as jnp
from jax import lax
from jax.experimental import pallas as pl
from jax.experimental.pallas import tpu as pltpu
from jax.sharding import PartitionSpec as P

VMEM = pl.BlockSpec(memory_space=pltpu.VMEM)
SMEM = pl.BlockSpec(memory_space=pltpu.SMEM)
ANY = pl.BlockSpec(memory_space=pl.ANY)
LINK = jnp.bfloat16
STEP = pl.CostEstimate(flops=3 * 10**9, bytes_accessed=3 * 10**6, transcendentals=0)
COSTLY = pl.CostEstimate(flops=10**10, bytes_accessed=10**7, transcendentals=0)


def params():
    return pltpu.CompilerParams(vmem_limit_bytes=24 << 20)


def in_hbm(x):
    return pltpu.with_memory_space_constraint(x, pltpu.HBM)


def unroll_of(caps, most):
    return next((u for u in range(min(most, caps), 0, -1) if caps % u == 0), 0)


def add_list(table, rep, src, left, right_t, wave, acc, begin=0, end=None):
    end = table.shape[-1] if end is None else end
    unroll = unroll_of(end - begin, 64)

    def body(step, carry):
        slots = [begin + step * unroll + q for q in range(unroll)]
        terms = [table[0, 0, 0, rep, src, c] for c in slots]
        inner = [
            jnp.dot(
                left[terms[q]],
                wave[table[2, 0, 0, rep, src, slots[q]]],
                preferred_element_type=jnp.float32,
            ).astype(jnp.bfloat16)
            for q in range(unroll)
        ]
        outer = [
            jnp.dot(inner[q], right_t[terms[q]], preferred_element_type=jnp.float32)
            for q in range(unroll)
        ]
        for q in range(unroll):
            acc[table[1, 0, 0, rep, src, slots[q]]] += outer[q]
        return carry

    if unroll:
        lax.fori_loop(0, (end - begin) // unroll, body, 0)


def load_kernel(
    order, left, right, wave, table,
    left_rows, right_t, wave_here, table_here, right_here, sems,
):
    rep, op = lax.axis_index("rep"), lax.axis_index("op")
    rows = left_rows.shape[1] // len(order)
    count = right_t.shape[0]
    part = next(p for p in (8, 4, 2, 1) if count % p == 0)
    moves = [(table, table_here)]
    for k in range(0, count, part):
        moves.append((right.at[pl.ds(k, part)], right_here.at[pl.ds(k, part)]))
    for g, s in enumerate(order):
        first = pl.multiple_of((jnp.bitwise_xor(op, s) * 2 + rep) * rows, rows)
        moves.append((left.at[:, pl.ds(first, rows), :], left_rows.at[:, pl.ds(g * rows, rows), :]))
    moves.append((wave, wave_here))
    copies = [pltpu.make_async_copy(a, b, sems.at[i]) for i, (a, b) in enumerate(moves)]
    for copy in copies:
        copy.start()
    copies[0].wait()
    for k in range(count):
        if k % part == 0:
            copies[1 + k // part].wait()
        right_t[k] = right_here[k].T
    for copy in copies[1 + count // part :]:
        copy.wait()


def split_rows(acc, outs):
    first = 0
    for out in outs:
        tiles, rows, _ = out.shape[-3:]
        for to in [out] if len(out.shape) == 3 else [out.at[g] for g in range(out.shape[0])]:
            to[...] = acc[0:tiles, first : first + rows, :].astype(out.dtype)
            first += rows


def other_kernel(
    early, other, table, left_rows, right_t, wave, own_acc, other_here, acc, sem
):
    rep, blk = lax.axis_index("rep"), lax.axis_index("blk")
    copy = pltpu.make_async_copy(other, other_here, sem)
    copy.start()
    own_acc[...] = jnp.zeros_like(own_acc)
    acc[...] = jnp.zeros_like(acc)
    add_list(table, rep, blk, left_rows, right_t, wave, own_acc, 0, early)
    copy.wait()
    add_list(other_here, rep, blk, left_rows, right_t, wave, acc)


def pair_kernel(table, left_rows, right_t, wave_pair, start, *refs):
    *outs, acc = refs
    acc[...] = start[...]
    rep, blk = lax.axis_index("rep"), lax.axis_index("blk")
    add_list(table, 1 - rep, blk, left_rows, right_t, wave_pair, acc)
    split_rows(acc, outs)


def own_kernel(early, table, left_rows, right_t, wave, wave_pair, start, acc):
    acc[...] = start[...]
    rep, blk = lax.axis_index("rep"), lax.axis_index("blk")
    add_list(table, rep, blk, left_rows, right_t, wave, acc, early)
    add_list(table, 1 - rep, blk, left_rows, right_t, wave_pair, acc)


def add_block(acc, block, got, out):
    tiles, rows, _ = out.shape
    kept = acc[0:tiles, block * rows : (block + 1) * rows, :]
    out[...] = (kept + got[...].astype(jnp.float32)).astype(out.dtype)


def sum_kernel(block, acc, got, *refs):
    add_block(acc, block, got, refs[-1])


def cut_kernel(block, acc, before, out):
    del before
    tiles, rows, _ = out.shape
    out[...] = acc[0:tiles, block * rows : (block + 1) * rows, :].astype(out.dtype)


def pair_sum_kernel(kept, got, before, out):
    del before
    out[...] = (kept[...] + got[...].astype(jnp.float32)).astype(out.dtype)


def more_kernel(so_far, got, out):
    out[...] = so_far[...] + got[...].astype(jnp.float32)


def final_kernel(so_far, got, out):
    total = so_far[...] + got[...].astype(jnp.float32)
    for t in range(total.shape[0]):
        out[:, t, :] = total[t]


def call(kernel, out_shape, args, ins, outs, **kwargs):
    return pl.pallas_call(
        kernel, out_shape=out_shape, in_specs=ins, out_specs=outs, compiler_params=params(), **kwargs
    )(*args)


def at_source(wavefunction, left_env, right_env, slot_table):
    tiles_dev, width, _ = wavefunction.shape
    terms, row_total, _ = left_env.shape
    op_count = lax.axis_size("op")
    tiles = 2 * tiles_dev
    rows = row_total // (2 * op_count)
    order = [*range(op_count // 2, op_count), *range(op_count // 2 - 1, -1, -1)]
    swap = [(0, 1), (1, 0)]
    f32 = jnp.float32
    shape = jax.ShapeDtypeStruct
    table_spec = pltpu.SMEM(slot_table.shape, slot_table.dtype)
    block = (tiles, rows, width)

    across = [(0, 3), (1, 2), (2, 1), (3, 0)]
    table_other = lax.ppermute(slot_table, ("blk", "rep"), across)
    wave_pair = lax.ppermute(wavefunction, "rep", swap)
    acc_shape = shape((tiles + 1, op_count * rows, width), f32)
    caps = slot_table.shape[-1]
    early = caps // 8
    left_shape = shape((terms, op_count * rows, width), left_env.dtype)
    left_rows, right_t, wave, own_table = call(
        functools.partial(load_kernel, order),
        (
            left_shape,
            shape(right_env.shape, right_env.dtype),
            shape(wavefunction.shape, wavefunction.dtype),
            table_spec,
        ),
        [in_hbm(x) for x in (left_env, right_env, wavefunction, slot_table)],
        [ANY] * 4,
        (VMEM, VMEM, VMEM, SMEM),
        scratch_shapes=[
            pltpu.VMEM(right_env.shape, right_env.dtype),
            pltpu.SemaphoreType.DMA((2 + op_count + terms,)),
        ],
    )
    acc, other_table, acc_other = call(
        functools.partial(other_kernel, early),
        (acc_shape, table_spec, acc_shape),
        (table_other, own_table, left_rows, right_t, wave),
        [ANY, SMEM] + [VMEM] * 3,
        (VMEM, SMEM, VMEM),
        scratch_shapes=[pltpu.SemaphoreType.DMA],
        cost_estimate=COSTLY,
    )
    sends = call(
        pair_kernel,
        (shape(block, LINK),) * (op_count - 1) + (shape(block, f32),),
        (other_table, left_rows, right_t, wave_pair, acc_other),
        [SMEM] + [VMEM] * 4,
        (VMEM,) * op_count,
        scratch_shapes=[pltpu.VMEM(acc_shape.shape, f32)],
    )

    def to_blk(x):
        return lax.ppermute(x, "blk", swap)

    def to_op(x, s):
        return lax.ppermute(x, "op", [(i, i ^ s) for i in range(op_count)])

    *far, near, own = sends
    got = [to_blk(x) for x in far]
    got_near = to_op(near, order[-2])
    acc = call(
        functools.partial(own_kernel, early),
        acc_shape,
        (own_table, left_rows, right_t, wave, wave_pair, acc),
        [SMEM] + [VMEM] * 5,
        VMEM,
    )
    total = call(
        functools.partial(sum_kernel, 0),
        shape(block, LINK),
        (acc, got[0]),
        [VMEM] * 2,
        VMEM,
    )
    arrived = [to_op(total, order[0])]
    near = call(
        functools.partial(cut_kernel, op_count - 2),
        shape(block, LINK),
        (acc, total),
        [VMEM, ANY],
        VMEM,
    )
    arrived.append(to_op(near, order[-2]))
    total = call(
        functools.partial(sum_kernel, 1),
        shape(block, LINK),
        (acc, got[1], near),
        [VMEM] * 2 + [ANY],
        VMEM,
    )
    arrived.append(to_op(total, order[1]))
    own = call(
        pair_sum_kernel,
        shape(block, LINK),
        (own, got_near, total),
        [VMEM] * 2 + [ANY],
        VMEM,
    )
    here = to_blk(own)
    so_far = call(
        functools.partial(sum_kernel, op_count - 1),
        shape(block, f32),
        (acc, arrived[0]),
        [VMEM] * 2,
        VMEM,
        cost_estimate=STEP,
    )
    for x in arrived[1:]:
        so_far = call(
            more_kernel, shape(block, f32), (so_far, x), [VMEM] * 2, VMEM, cost_estimate=STEP
        )
    return call(
        final_kernel,
        shape((rows, tiles, width), f32),
        (so_far, here),
        [VMEM] * 2,
        VMEM,
    )


def list_kernel(where, table, left, right, wave, start, acc):
    acc[...] = start[...]
    add_list(table, where[0], where[1], left, right, wave, acc)


def gathered(wavefunction, left_env, right_env, slot_table):
    tiles_dev, width, _ = wavefunction.shape
    blk_count = lax.axis_size("blk")
    tiles_blk = tiles_dev * lax.axis_size("rep")
    rep, blk = lax.axis_index("rep"), lax.axis_index("blk")
    right_t = jnp.swapaxes(right_env, 1, 2)
    acc = jnp.zeros((tiles_blk + 1, left_env.shape[1], width), jnp.float32)
    for s in range(blk_count):
        pairs = [((i + s) % blk_count, i) for i in range(blk_count)]
        acc = call(
            list_kernel,
            jax.ShapeDtypeStruct(acc.shape, acc.dtype),
            (
                jnp.stack([rep, (blk + s) % blk_count]).astype(jnp.int32),
                slot_table,
                left_env,
                right_t,
                lax.ppermute(wavefunction, "blk", pairs) if s else wavefunction,
                acc,
            ),
            [SMEM] * 2 + [VMEM] * 4,
            VMEM,
        )
    partial = jnp.swapaxes(acc[:tiles_blk], 0, 1)
    return lax.psum_scatter(partial, ("op", "rep"), scatter_dimension=0, tiled=True)


def shards(wavefunction, left_env, right_env, slot_table):
    op_count = lax.axis_size("op")
    rows = left_env.shape[1] // (2 * op_count)
    fits = lax.axis_size("rep") == 2 and lax.axis_size("blk") == 2
    fits = fits and op_count > 2 and op_count & (op_count - 1) == 0
    fits = fits and rows % 16 == 0 and rows * 2 * op_count == left_env.shape[1]
    form = at_source if fits else gathered
    return form(wavefunction, left_env, right_env, slot_table)


def solution(mesh):
    placed = (
        P(("grp", "blk", "rep"), None, None),
        P(("grp", "op"), None, None),
        P(("grp", "op"), None, None),
        P(None, "op", "blk", None, None, None),
    )
    return jax.shard_map(
        shards,
        mesh=mesh,
        in_specs=placed,
        out_specs=P(("op", "rep"), ("grp", "blk"), None),
        check_vma=False,
    )
```

```python
import functools

import jax
import jax.numpy as jnp
from jax import lax
from jax.experimental import pallas as pl
from jax.experimental.pallas import tpu as pltpu
from jax.sharding import PartitionSpec as P

VMEM = pl.BlockSpec(memory_space=pltpu.VMEM)
SMEM = pl.BlockSpec(memory_space=pltpu.SMEM)
ANY = pl.BlockSpec(memory_space=pl.ANY)
LINK = jnp.bfloat16
STEP = pl.CostEstimate(flops=3 * 10**9, bytes_accessed=3 * 10**6, transcendentals=0)
COSTLY = pl.CostEstimate(flops=10**10, bytes_accessed=10**7, transcendentals=0)


def params():
    return pltpu.CompilerParams(vmem_limit_bytes=24 << 20)


def in_hbm(x):
    return pltpu.with_memory_space_constraint(x, pltpu.HBM)


def unroll_of(caps, most):
    return next((u for u in range(min(most, caps), 0, -1) if caps % u == 0), 0)


def add_list(table, rep, src, left, right_t, wave, acc, begin=0, end=None):
    end = table.shape[-1] if end is None else end
    unroll = unroll_of(end - begin, 64)

    def body(step, carry):
        slots = [begin + step * unroll + q for q in range(unroll)]
        terms = [table[0, 0, 0, rep, src, c] for c in slots]
        inner = [
            jnp.dot(
                left[terms[q]],
                wave[table[2, 0, 0, rep, src, slots[q]]],
                preferred_element_type=jnp.float32,
            ).astype(jnp.bfloat16)
            for q in range(unroll)
        ]
        outer = [
            jnp.dot(inner[q], right_t[terms[q]], preferred_element_type=jnp.float32)
            for q in range(unroll)
        ]
        for q in range(unroll):
            acc[table[1, 0, 0, rep, src, slots[q]]] += outer[q]
        return carry

    if unroll:
        lax.fori_loop(0, (end - begin) // unroll, body, 0)


def load_kernel(
    order, left, right, wave, table,
    left_rows, right_t, wave_here, table_here, right_here, sems,
):
    rep, op = lax.axis_index("rep"), lax.axis_index("op")
    rows = left_rows.shape[1] // len(order)
    count = right_t.shape[0]
    part = next(p for p in (8, 4, 2, 1) if count % p == 0)
    moves = [(table, table_here)]
    for k in range(0, count, part):
        moves.append((right.at[pl.ds(k, part)], right_here.at[pl.ds(k, part)]))
    for g, s in enumerate(order):
        first = pl.multiple_of((jnp.bitwise_xor(op, s) * 2 + rep) * rows, rows)
        moves.append((left.at[:, pl.ds(first, rows), :], left_rows.at[:, pl.ds(g * rows, rows), :]))
    moves.append((wave, wave_here))
    copies = [pltpu.make_async_copy(a, b, sems.at[i]) for i, (a, b) in enumerate(moves)]
    for copy in copies:
        copy.start()
    copies[0].wait()
    for k in range(count):
        if k % part == 0:
            copies[1 + k // part].wait()
        right_t[k] = right_here[k].T
    for copy in copies[1 + count // part :]:
        copy.wait()


def split_rows(acc, outs):
    first = 0
    for out in outs:
        tiles, rows, _ = out.shape[-3:]
        for to in [out] if len(out.shape) == 3 else [out.at[g] for g in range(out.shape[0])]:
            to[...] = acc[0:tiles, first : first + rows, :].astype(out.dtype)
            first += rows


def other_kernel(
    other, left_rows, right_t, wave, other_here, acc, sem
):
    rep, blk = lax.axis_index("rep"), lax.axis_index("blk")
    copy = pltpu.make_async_copy(other, other_here, sem)
    copy.start()
    acc[...] = jnp.zeros_like(acc)
    copy.wait()
    add_list(other_here, rep, blk, left_rows, right_t, wave, acc)


def pair_kernel(table, left_rows, right_t, wave_pair, start, *refs):
    *outs, acc = refs
    acc[...] = start[...]
    rep, blk = lax.axis_index("rep"), lax.axis_index("blk")
    add_list(table, 1 - rep, blk, left_rows, right_t, wave_pair, acc)
    split_rows(acc, outs)


def own_kernel(table, left_rows, right_t, wave, wave_pair, acc):
    acc[...] = jnp.zeros_like(acc)
    rep, blk = lax.axis_index("rep"), lax.axis_index("blk")
    add_list(table, rep, blk, left_rows, right_t, wave, acc)
    add_list(table, 1 - rep, blk, left_rows, right_t, wave_pair, acc)


def add_block(acc, block, got, out):
    tiles, rows, _ = out.shape
    kept = acc[0:tiles, block * rows : (block + 1) * rows, :]
    out[...] = (kept + got[...].astype(jnp.float32)).astype(out.dtype)


def sum_kernel(block, acc, got, *refs):
    add_block(acc, block, got, refs[-1])


def cut_kernel(block, acc, before, out):
    del before
    tiles, rows, _ = out.shape
    out[...] = acc[0:tiles, block * rows : (block + 1) * rows, :].astype(out.dtype)


def pair_sum_kernel(kept, got, before, out):
    del before
    out[...] = (kept[...] + got[...].astype(jnp.float32)).astype(out.dtype)


def more_kernel(so_far, got, out):
    out[...] = so_far[...] + got[...].astype(jnp.float32)


def final_kernel(so_far, got, out):
    total = so_far[...] + got[...].astype(jnp.float32)
    for t in range(total.shape[0]):
        out[:, t, :] = total[t]


def call(kernel, out_shape, args, ins, outs, **kwargs):
    return pl.pallas_call(
        kernel, out_shape=out_shape, in_specs=ins, out_specs=outs, compiler_params=params(), **kwargs
    )(*args)


def at_source(wavefunction, left_env, right_env, slot_table):
    tiles_dev, width, _ = wavefunction.shape
    terms, row_total, _ = left_env.shape
    op_count = lax.axis_size("op")
    tiles = 2 * tiles_dev
    rows = row_total // (2 * op_count)
    order = [*range(op_count // 2, op_count), *range(op_count // 2 - 1, -1, -1)]
    swap = [(0, 1), (1, 0)]
    f32 = jnp.float32
    shape = jax.ShapeDtypeStruct
    table_spec = pltpu.SMEM(slot_table.shape, slot_table.dtype)
    block = (tiles, rows, width)

    across = [(0, 3), (1, 2), (2, 1), (3, 0)]
    table_other = lax.ppermute(slot_table, ("blk", "rep"), across)
    wave_pair = lax.ppermute(wavefunction, "rep", swap)
    acc_shape = shape((tiles + 1, op_count * rows, width), f32)
    left_shape = shape((terms, op_count * rows, width), left_env.dtype)
    left_rows, right_t, wave, own_table = call(
        functools.partial(load_kernel, order),
        (
            left_shape,
            shape(right_env.shape, right_env.dtype),
            shape(wavefunction.shape, wavefunction.dtype),
            table_spec,
        ),
        [in_hbm(x) for x in (left_env, right_env, wavefunction, slot_table)],
        [ANY] * 4,
        (VMEM, VMEM, VMEM, SMEM),
        scratch_shapes=[
            pltpu.VMEM(right_env.shape, right_env.dtype),
            pltpu.SemaphoreType.DMA((2 + op_count + terms,)),
        ],
    )
    other_table, acc_other = call(
        other_kernel,
        (table_spec, acc_shape),
        (table_other, left_rows, right_t, wave),
        [ANY] + [VMEM] * 3,
        (SMEM, VMEM),
        scratch_shapes=[pltpu.SemaphoreType.DMA],
        cost_estimate=COSTLY,
    )
    sends = call(
        pair_kernel,
        (shape(block, LINK),) * (op_count - 1) + (shape(block, f32),),
        (other_table, left_rows, right_t, wave_pair, acc_other),
        [SMEM] + [VMEM] * 4,
        (VMEM,) * op_count,
        scratch_shapes=[pltpu.VMEM(acc_shape.shape, f32)],
    )

    def to_blk(x):
        return lax.ppermute(x, "blk", swap)

    def to_op(x, s):
        return lax.ppermute(x, "op", [(i, i ^ s) for i in range(op_count)])

    *far, near, own = sends
    got = [to_blk(x) for x in far]
    got_near = to_op(near, order[-2])
    acc = call(
        own_kernel,
        acc_shape,
        (own_table, left_rows, right_t, wave, wave_pair),
        [SMEM] + [VMEM] * 4,
        VMEM,
    )
    total = call(
        functools.partial(sum_kernel, 0),
        shape(block, LINK),
        (acc, got[0]),
        [VMEM] * 2,
        VMEM,
    )
    arrived = [to_op(total, order[0])]
    near = call(
        functools.partial(cut_kernel, op_count - 2),
        shape(block, LINK),
        (acc, total),
        [VMEM, ANY],
        VMEM,
    )
    arrived.append(to_op(near, order[-2]))
    total = call(
        functools.partial(sum_kernel, 1),
        shape(block, LINK),
        (acc, got[1], near),
        [VMEM] * 2 + [ANY],
        VMEM,
    )
    arrived.append(to_op(total, order[1]))
    own = call(
        pair_sum_kernel,
        shape(block, LINK),
        (own, got_near, total),
        [VMEM] * 2 + [ANY],
        VMEM,
    )
    here = to_blk(own)
    so_far = call(
        functools.partial(sum_kernel, op_count - 1),
        shape(block, f32),
        (acc, arrived[0]),
        [VMEM] * 2,
        VMEM,
        cost_estimate=STEP,
    )
    for x in arrived[1:]:
        so_far = call(
            more_kernel, shape(block, f32), (so_far, x), [VMEM] * 2, VMEM, cost_estimate=STEP
        )
    return call(
        final_kernel,
        shape((rows, tiles, width), f32),
        (so_far, here),
        [VMEM] * 2,
        VMEM,
    )


def list_kernel(where, table, left, right, wave, start, acc):
    acc[...] = start[...]
    add_list(table, where[0], where[1], left, right, wave, acc)


def gathered(wavefunction, left_env, right_env, slot_table):
    tiles_dev, width, _ = wavefunction.shape
    blk_count = lax.axis_size("blk")
    tiles_blk = tiles_dev * lax.axis_size("rep")
    rep, blk = lax.axis_index("rep"), lax.axis_index("blk")
    right_t = jnp.swapaxes(right_env, 1, 2)
    acc = jnp.zeros((tiles_blk + 1, left_env.shape[1], width), jnp.float32)
    for s in range(blk_count):
        pairs = [((i + s) % blk_count, i) for i in range(blk_count)]
        acc = call(
            list_kernel,
            jax.ShapeDtypeStruct(acc.shape, acc.dtype),
            (
                jnp.stack([rep, (blk + s) % blk_count]).astype(jnp.int32),
                slot_table,
                left_env,
                right_t,
                lax.ppermute(wavefunction, "blk", pairs) if s else wavefunction,
                acc,
            ),
            [SMEM] * 2 + [VMEM] * 4,
            VMEM,
        )
    partial = jnp.swapaxes(acc[:tiles_blk], 0, 1)
    return lax.psum_scatter(partial, ("op", "rep"), scatter_dimension=0, tiled=True)


def shards(wavefunction, left_env, right_env, slot_table):
    op_count = lax.axis_size("op")
    rows = left_env.shape[1] // (2 * op_count)
    fits = lax.axis_size("rep") == 2 and lax.axis_size("blk") == 2
    fits = fits and op_count > 2 and op_count & (op_count - 1) == 0
    fits = fits and rows % 16 == 0 and rows * 2 * op_count == left_env.shape[1]
    form = at_source if fits else gathered
    return form(wavefunction, left_env, right_env, slot_table)


def solution(mesh):
    placed = (
        P(("grp", "blk", "rep"), None, None),
        P(("grp", "op"), None, None),
        P(("grp", "op"), None, None),
        P(None, "op", "blk", None, None, None),
    )
    return jax.shard_map(
        shards,
        mesh=mesh,
        in_specs=placed,
        out_specs=P(("op", "rep"), ("grp", "blk"), None),
        check_vma=False,
    )
```

```python
import functools

import jax
import jax.numpy as jnp
from jax import lax
from jax.experimental import pallas as pl
from jax.experimental.pallas import tpu as pltpu
from jax.sharding import PartitionSpec as P

VMEM = pl.BlockSpec(memory_space=pltpu.VMEM)
SMEM = pl.BlockSpec(memory_space=pltpu.SMEM)
ANY = pl.BlockSpec(memory_space=pl.ANY)
LINK = jnp.bfloat16
BEHIND = 16
STEP = pl.CostEstimate(flops=3 * 10**9, bytes_accessed=3 * 10**6, transcendentals=0)
COSTLY = pl.CostEstimate(flops=10**10, bytes_accessed=10**7, transcendentals=0)


def params():
    return pltpu.CompilerParams(vmem_limit_bytes=24 << 20)


def in_hbm(x):
    return pltpu.with_memory_space_constraint(x, pltpu.HBM)


def unroll_of(caps, most):
    return next((u for u in range(min(most, caps), 0, -1) if caps % u == 0), 0)


def add_list(table, rep, src, left, right_t, wave, acc, begin=0, end=None):
    end = table.shape[-1] if end is None else end
    unroll = unroll_of(end - begin, 64)

    def body(step, carry):
        slots = [begin + step * unroll + q for q in range(unroll)]
        terms = [table[0, 0, 0, rep, src, c] for c in slots]
        inner = {}
        for q in range(unroll + BEHIND):
            if q < unroll:
                inner[q] = jnp.dot(
                    left[terms[q]],
                    wave[table[2, 0, 0, rep, src, slots[q]]],
                    preferred_element_type=jnp.float32,
                ).astype(jnp.bfloat16)
            p = q - BEHIND
            if p >= 0:
                acc[table[1, 0, 0, rep, src, slots[p]]] += jnp.dot(
                    inner.pop(p), right_t[terms[p]], preferred_element_type=jnp.float32
                )
        return carry

    if unroll:
        lax.fori_loop(0, (end - begin) // unroll, body, 0)


def load_kernel(
    order, left, right, wave, table,
    left_rows, right_t, wave_here, table_here, right_here, sems,
):
    rep, op = lax.axis_index("rep"), lax.axis_index("op")
    rows = left_rows.shape[1] // len(order)
    count = right_t.shape[0]
    part = next(p for p in (8, 4, 2, 1) if count % p == 0)
    moves = [(table, table_here)]
    for k in range(0, count, part):
        moves.append((right.at[pl.ds(k, part)], right_here.at[pl.ds(k, part)]))
    for g, s in enumerate(order):
        first = pl.multiple_of((jnp.bitwise_xor(op, s) * 2 + rep) * rows, rows)
        moves.append((left.at[:, pl.ds(first, rows), :], left_rows.at[:, pl.ds(g * rows, rows), :]))
    moves.append((wave, wave_here))
    copies = [pltpu.make_async_copy(a, b, sems.at[i]) for i, (a, b) in enumerate(moves)]
    for copy in copies:
        copy.start()
    copies[0].wait()
    for k in range(count):
        if k % part == 0:
            copies[1 + k // part].wait()
        right_t[k] = right_here[k].T
    for copy in copies[1 + count // part :]:
        copy.wait()


def split_rows(acc, outs):
    first = 0
    for out in outs:
        tiles, rows, _ = out.shape[-3:]
        for to in [out] if len(out.shape) == 3 else [out.at[g] for g in range(out.shape[0])]:
            to[...] = acc[0:tiles, first : first + rows, :].astype(out.dtype)
            first += rows


def other_kernel(
    other, left_rows, right_t, wave, other_here, acc, sem
):
    rep, blk = lax.axis_index("rep"), lax.axis_index("blk")
    copy = pltpu.make_async_copy(other, other_here, sem)
    copy.start()
    acc[...] = jnp.zeros_like(acc)
    copy.wait()
    add_list(other_here, rep, blk, left_rows, right_t, wave, acc)


def pair_kernel(table, left_rows, right_t, wave_pair, start, *refs):
    *outs, acc = refs
    acc[...] = start[...]
    rep, blk = lax.axis_index("rep"), lax.axis_index("blk")
    add_list(table, 1 - rep, blk, left_rows, right_t, wave_pair, acc)
    split_rows(acc, outs)


def own_kernel(table, left_rows, right_t, wave, wave_pair, acc):
    acc[...] = jnp.zeros_like(acc)
    rep, blk = lax.axis_index("rep"), lax.axis_index("blk")
    add_list(table, rep, blk, left_rows, right_t, wave, acc)
    add_list(table, 1 - rep, blk, left_rows, right_t, wave_pair, acc)


def add_block(acc, block, got, out):
    tiles, rows, _ = out.shape
    kept = acc[0:tiles, block * rows : (block + 1) * rows, :]
    out[...] = (kept + got[...].astype(jnp.float32)).astype(out.dtype)


def sum_kernel(block, acc, got, *refs):
    add_block(acc, block, got, refs[-1])


def cut_kernel(block, acc, before, out):
    del before
    tiles, rows, _ = out.shape
    out[...] = acc[0:tiles, block * rows : (block + 1) * rows, :].astype(out.dtype)


def pair_sum_kernel(kept, got, before, out):
    del before
    out[...] = (kept[...] + got[...].astype(jnp.float32)).astype(out.dtype)


def more_kernel(so_far, got, out):
    out[...] = so_far[...] + got[...].astype(jnp.float32)


def final_kernel(so_far, got, out):
    total = so_far[...] + got[...].astype(jnp.float32)
    for t in range(total.shape[0]):
        out[:, t, :] = total[t]


def call(kernel, out_shape, args, ins, outs, **kwargs):
    return pl.pallas_call(
        kernel, out_shape=out_shape, in_specs=ins, out_specs=outs, compiler_params=params(), **kwargs
    )(*args)


def at_source(wavefunction, left_env, right_env, slot_table):
    tiles_dev, width, _ = wavefunction.shape
    terms, row_total, _ = left_env.shape
    op_count = lax.axis_size("op")
    tiles = 2 * tiles_dev
    rows = row_total // (2 * op_count)
    order = [*range(op_count // 2, op_count), *range(op_count // 2 - 1, -1, -1)]
    swap = [(0, 1), (1, 0)]
    f32 = jnp.float32
    shape = jax.ShapeDtypeStruct
    table_spec = pltpu.SMEM(slot_table.shape, slot_table.dtype)
    block = (tiles, rows, width)

    across = [(0, 3), (1, 2), (2, 1), (3, 0)]
    table_other = lax.ppermute(slot_table, ("blk", "rep"), across)
    wave_pair = lax.ppermute(wavefunction, "rep", swap)
    acc_shape = shape((tiles + 1, op_count * rows, width), f32)
    left_shape = shape((terms, op_count * rows, width), left_env.dtype)
    left_rows, right_t, wave, own_table = call(
        functools.partial(load_kernel, order),
        (
            left_shape,
            shape(right_env.shape, right_env.dtype),
            shape(wavefunction.shape, wavefunction.dtype),
            table_spec,
        ),
        [in_hbm(x) for x in (left_env, right_env, wavefunction, slot_table)],
        [ANY] * 4,
        (VMEM, VMEM, VMEM, SMEM),
        scratch_shapes=[
            pltpu.VMEM(right_env.shape, right_env.dtype),
            pltpu.SemaphoreType.DMA((2 + op_count + terms,)),
        ],
    )
    other_table, acc_other = call(
        other_kernel,
        (table_spec, acc_shape),
        (table_other, left_rows, right_t, wave),
        [ANY] + [VMEM] * 3,
        (SMEM, VMEM),
        scratch_shapes=[pltpu.SemaphoreType.DMA],
        cost_estimate=COSTLY,
    )
    sends = call(
        pair_kernel,
        (shape(block, LINK),) * (op_count - 1) + (shape(block, f32),),
        (other_table, left_rows, right_t, wave_pair, acc_other),
        [SMEM] + [VMEM] * 4,
        (VMEM,) * op_count,
        scratch_shapes=[pltpu.VMEM(acc_shape.shape, f32)],
    )

    def to_blk(x):
        return lax.ppermute(x, "blk", swap)

    def to_op(x, s):
        return lax.ppermute(x, "op", [(i, i ^ s) for i in range(op_count)])

    *far, near, own = sends
    got = [to_blk(x) for x in far]
    got_near = to_op(near, order[-2])
    acc = call(
        own_kernel,
        acc_shape,
        (own_table, left_rows, right_t, wave, wave_pair),
        [SMEM] + [VMEM] * 4,
        VMEM,
    )
    total = call(
        functools.partial(sum_kernel, 0),
        shape(block, LINK),
        (acc, got[0]),
        [VMEM] * 2,
        VMEM,
    )
    arrived = [to_op(total, order[0])]
    near = call(
        functools.partial(cut_kernel, op_count - 2),
        shape(block, LINK),
        (acc, total),
        [VMEM, ANY],
        VMEM,
    )
    arrived.append(to_op(near, order[-2]))
    total = call(
        functools.partial(sum_kernel, 1),
        shape(block, LINK),
        (acc, got[1], near),
        [VMEM] * 2 + [ANY],
        VMEM,
    )
    arrived.append(to_op(total, order[1]))
    own = call(
        pair_sum_kernel,
        shape(block, LINK),
        (own, got_near, total),
        [VMEM] * 2 + [ANY],
        VMEM,
    )
    here = to_blk(own)
    so_far = call(
        functools.partial(sum_kernel, op_count - 1),
        shape(block, f32),
        (acc, arrived[0]),
        [VMEM] * 2,
        VMEM,
        cost_estimate=STEP,
    )
    for x in arrived[1:]:
        so_far = call(
            more_kernel, shape(block, f32), (so_far, x), [VMEM] * 2, VMEM, cost_estimate=STEP
        )
    return call(
        final_kernel,
        shape((rows, tiles, width), f32),
        (so_far, here),
        [VMEM] * 2,
        VMEM,
    )


def list_kernel(where, table, left, right, wave, start, acc):
    acc[...] = start[...]
    add_list(table, where[0], where[1], left, right, wave, acc)


def gathered(wavefunction, left_env, right_env, slot_table):
    tiles_dev, width, _ = wavefunction.shape
    blk_count = lax.axis_size("blk")
    tiles_blk = tiles_dev * lax.axis_size("rep")
    rep, blk = lax.axis_index("rep"), lax.axis_index("blk")
    right_t = jnp.swapaxes(right_env, 1, 2)
    acc = jnp.zeros((tiles_blk + 1, left_env.shape[1], width), jnp.float32)
    for s in range(blk_count):
        pairs = [((i + s) % blk_count, i) for i in range(blk_count)]
        acc = call(
            list_kernel,
            jax.ShapeDtypeStruct(acc.shape, acc.dtype),
            (
                jnp.stack([rep, (blk + s) % blk_count]).astype(jnp.int32),
                slot_table,
                left_env,
                right_t,
                lax.ppermute(wavefunction, "blk", pairs) if s else wavefunction,
                acc,
            ),
            [SMEM] * 2 + [VMEM] * 4,
            VMEM,
        )
    partial = jnp.swapaxes(acc[:tiles_blk], 0, 1)
    return lax.psum_scatter(partial, ("op", "rep"), scatter_dimension=0, tiled=True)


def shards(wavefunction, left_env, right_env, slot_table):
    op_count = lax.axis_size("op")
    rows = left_env.shape[1] // (2 * op_count)
    fits = lax.axis_size("rep") == 2 and lax.axis_size("blk") == 2
    fits = fits and op_count > 2 and op_count & (op_count - 1) == 0
    fits = fits and rows % 16 == 0 and rows * 2 * op_count == left_env.shape[1]
    form = at_source if fits else gathered
    return form(wavefunction, left_env, right_env, slot_table)


def solution(mesh):
    placed = (
        P(("grp", "blk", "rep"), None, None),
        P(("grp", "op"), None, None),
        P(("grp", "op"), None, None),
        P(None, "op", "blk", None, None, None),
    )
    return jax.shard_map(
        shards,
        mesh=mesh,
        in_specs=placed,
        out_specs=P(("op", "rep"), ("grp", "blk"), None),
        check_vma=False,
    )
```

```python
import functools

import jax
import jax.numpy as jnp
from jax import lax
from jax.experimental import pallas as pl
from jax.experimental.pallas import tpu as pltpu
from jax.sharding import PartitionSpec as P

VMEM = pl.BlockSpec(memory_space=pltpu.VMEM)
SMEM = pl.BlockSpec(memory_space=pltpu.SMEM)
ANY = pl.BlockSpec(memory_space=pl.ANY)
LINK = jnp.bfloat16
BEHIND = 16
STEP = pl.CostEstimate(flops=3 * 10**9, bytes_accessed=3 * 10**6, transcendentals=0)
COSTLY = pl.CostEstimate(flops=10**10, bytes_accessed=10**7, transcendentals=0)


def params():
    return pltpu.CompilerParams(vmem_limit_bytes=24 << 20)


def in_hbm(x):
    return pltpu.with_memory_space_constraint(x, pltpu.HBM)


def unroll_of(caps, most):
    return next((u for u in range(min(most, caps), 0, -1) if caps % u == 0), 0)


def add_list(table, rep, src, left, right_t, wave, acc, begin=0, end=None):
    end = table.shape[-1] if end is None else end
    unroll = unroll_of(end - begin, 64)

    def body(step, carry):
        slots = [begin + step * unroll + q for q in range(unroll)]
        terms = [table[0, 0, 0, rep, src, c] for c in slots]
        inner = {}
        for q in range(unroll + BEHIND):
            if q < unroll:
                inner[q] = jnp.dot(
                    left[terms[q]],
                    wave[table[2, 0, 0, rep, src, slots[q]]],
                    preferred_element_type=jnp.float32,
                ).astype(jnp.bfloat16)
            p = q - BEHIND
            if p >= 0:
                acc[table[1, 0, 0, rep, src, slots[p]]] += jnp.dot(
                    inner.pop(p), right_t[terms[p]], preferred_element_type=jnp.float32
                )
        return carry

    if unroll:
        lax.fori_loop(0, (end - begin) // unroll, body, 0)


def load_kernel(
    order, left, right, wave, table,
    left_rows, right_t, wave_here, table_here, right_here, sems,
):
    rep, op = lax.axis_index("rep"), lax.axis_index("op")
    rows = left_rows.shape[1] // len(order)
    count = right_t.shape[0]
    part = next(p for p in (16, 8, 4, 2, 1) if count % p == 0)
    moves = [(table, table_here)]
    for k in range(0, count, part):
        moves.append((right.at[pl.ds(k, part)], right_here.at[pl.ds(k, part)]))
    for g, s in enumerate(order):
        first = pl.multiple_of((jnp.bitwise_xor(op, s) * 2 + rep) * rows, rows)
        moves.append((left.at[:, pl.ds(first, rows), :], left_rows.at[:, pl.ds(g * rows, rows), :]))
    moves.append((wave, wave_here))
    copies = [pltpu.make_async_copy(a, b, sems.at[i]) for i, (a, b) in enumerate(moves)]
    for copy in copies:
        copy.start()
    copies[0].wait()
    for k in range(count):
        if k % part == 0:
            copies[1 + k // part].wait()
        right_t[k] = right_here[k].T
    for copy in copies[1 + count // part :]:
        copy.wait()


def split_rows(acc, outs):
    first = 0
    for out in outs:
        tiles, rows, _ = out.shape[-3:]
        for to in [out] if len(out.shape) == 3 else [out.at[g] for g in range(out.shape[0])]:
            to[...] = acc[0:tiles, first : first + rows, :].astype(out.dtype)
            first += rows


def other_kernel(
    other, left_rows, right_t, wave, other_here, acc, sem
):
    rep, blk = lax.axis_index("rep"), lax.axis_index("blk")
    copy = pltpu.make_async_copy(other, other_here, sem)
    copy.start()
    acc[...] = jnp.zeros_like(acc)
    copy.wait()
    add_list(other_here, rep, blk, left_rows, right_t, wave, acc)


def pair_kernel(table, left_rows, right_t, wave_pair, start, *refs):
    *outs, acc = refs
    acc[...] = start[...]
    rep, blk = lax.axis_index("rep"), lax.axis_index("blk")
    add_list(table, 1 - rep, blk, left_rows, right_t, wave_pair, acc)
    split_rows(acc, outs)


def own_kernel(table, left_rows, right_t, wave, wave_pair, acc):
    acc[...] = jnp.zeros_like(acc)
    rep, blk = lax.axis_index("rep"), lax.axis_index("blk")
    add_list(table, rep, blk, left_rows, right_t, wave, acc)
    add_list(table, 1 - rep, blk, left_rows, right_t, wave_pair, acc)


def add_block(acc, block, got, out):
    tiles, rows, _ = out.shape
    kept = acc[0:tiles, block * rows : (block + 1) * rows, :]
    out[...] = (kept + got[...].astype(jnp.float32)).astype(out.dtype)


def sum_kernel(block, acc, got, *refs):
    add_block(acc, block, got, refs[-1])


def cut_kernel(block, acc, before, out):
    del before
    tiles, rows, _ = out.shape
    out[...] = acc[0:tiles, block * rows : (block + 1) * rows, :].astype(out.dtype)


def pair_sum_kernel(kept, got, before, out):
    del before
    out[...] = (kept[...] + got[...].astype(jnp.float32)).astype(out.dtype)


def more_kernel(so_far, got, out):
    out[...] = so_far[...] + got[...].astype(jnp.float32)


def final_kernel(so_far, got, out):
    total = so_far[...] + got[...].astype(jnp.float32)
    for t in range(total.shape[0]):
        out[:, t, :] = total[t]


def call(kernel, out_shape, args, ins, outs, **kwargs):
    return pl.pallas_call(
        kernel, out_shape=out_shape, in_specs=ins, out_specs=outs, compiler_params=params(), **kwargs
    )(*args)


def at_source(wavefunction, left_env, right_env, slot_table):
    tiles_dev, width, _ = wavefunction.shape
    terms, row_total, _ = left_env.shape
    op_count = lax.axis_size("op")
    tiles = 2 * tiles_dev
    rows = row_total // (2 * op_count)
    order = [*range(op_count // 2, op_count), *range(op_count // 2 - 1, -1, -1)]
    swap = [(0, 1), (1, 0)]
    f32 = jnp.float32
    shape = jax.ShapeDtypeStruct
    table_spec = pltpu.SMEM(slot_table.shape, slot_table.dtype)
    block = (tiles, rows, width)

    across = [(0, 3), (1, 2), (2, 1), (3, 0)]
    table_other = lax.ppermute(slot_table, ("blk", "rep"), across)
    wave_pair = lax.ppermute(wavefunction, "rep", swap)
    acc_shape = shape((tiles + 1, op_count * rows, width), f32)
    left_shape = shape((terms, op_count * rows, width), left_env.dtype)
    left_rows, right_t, wave, own_table = call(
        functools.partial(load_kernel, order),
        (
            left_shape,
            shape(right_env.shape, right_env.dtype),
            shape(wavefunction.shape, wavefunction.dtype),
            table_spec,
        ),
        [in_hbm(x) for x in (left_env, right_env, wavefunction, slot_table)],
        [ANY] * 4,
        (VMEM, VMEM, VMEM, SMEM),
        scratch_shapes=[
            pltpu.VMEM(right_env.shape, right_env.dtype),
            pltpu.SemaphoreType.DMA((2 + op_count + terms,)),
        ],
    )
    other_table, acc_other = call(
        other_kernel,
        (table_spec, acc_shape),
        (table_other, left_rows, right_t, wave),
        [ANY] + [VMEM] * 3,
        (SMEM, VMEM),
        scratch_shapes=[pltpu.SemaphoreType.DMA],
        cost_estimate=COSTLY,
    )
    sends = call(
        pair_kernel,
        (shape(block, LINK),) * (op_count - 1) + (shape(block, f32),),
        (other_table, left_rows, right_t, wave_pair, acc_other),
        [SMEM] + [VMEM] * 4,
        (VMEM,) * op_count,
        scratch_shapes=[pltpu.VMEM(acc_shape.shape, f32)],
    )

    def to_blk(x):
        return lax.ppermute(x, "blk", swap)

    def to_op(x, s):
        return lax.ppermute(x, "op", [(i, i ^ s) for i in range(op_count)])

    *far, near, own = sends
    got = [to_blk(x) for x in far]
    got_near = to_op(near, order[-2])
    acc = call(
        own_kernel,
        acc_shape,
        (own_table, left_rows, right_t, wave, wave_pair),
        [SMEM] + [VMEM] * 4,
        VMEM,
    )
    total = call(
        functools.partial(sum_kernel, 0),
        shape(block, LINK),
        (acc, got[0]),
        [VMEM] * 2,
        VMEM,
    )
    arrived = [to_op(total, order[0])]
    near = call(
        functools.partial(cut_kernel, op_count - 2),
        shape(block, LINK),
        (acc, total),
        [VMEM, ANY],
        VMEM,
    )
    arrived.append(to_op(near, order[-2]))
    total = call(
        functools.partial(sum_kernel, 1),
        shape(block, LINK),
        (acc, got[1], near),
        [VMEM] * 2 + [ANY],
        VMEM,
    )
    arrived.append(to_op(total, order[1]))
    own = call(
        pair_sum_kernel,
        shape(block, LINK),
        (own, got_near, total),
        [VMEM] * 2 + [ANY],
        VMEM,
    )
    here = to_blk(own)
    so_far = call(
        functools.partial(sum_kernel, op_count - 1),
        shape(block, f32),
        (acc, arrived[0]),
        [VMEM] * 2,
        VMEM,
        cost_estimate=STEP,
    )
    for x in arrived[1:]:
        so_far = call(
            more_kernel, shape(block, f32), (so_far, x), [VMEM] * 2, VMEM, cost_estimate=STEP
        )
    return call(
        final_kernel,
        shape((rows, tiles, width), f32),
        (so_far, here),
        [VMEM] * 2,
        VMEM,
    )


def list_kernel(where, table, left, right, wave, start, acc):
    acc[...] = start[...]
    add_list(table, where[0], where[1], left, right, wave, acc)


def gathered(wavefunction, left_env, right_env, slot_table):
    tiles_dev, width, _ = wavefunction.shape
    blk_count = lax.axis_size("blk")
    tiles_blk = tiles_dev * lax.axis_size("rep")
    rep, blk = lax.axis_index("rep"), lax.axis_index("blk")
    right_t = jnp.swapaxes(right_env, 1, 2)
    acc = jnp.zeros((tiles_blk + 1, left_env.shape[1], width), jnp.float32)
    for s in range(blk_count):
        pairs = [((i + s) % blk_count, i) for i in range(blk_count)]
        acc = call(
            list_kernel,
            jax.ShapeDtypeStruct(acc.shape, acc.dtype),
            (
                jnp.stack([rep, (blk + s) % blk_count]).astype(jnp.int32),
                slot_table,
                left_env,
                right_t,
                lax.ppermute(wavefunction, "blk", pairs) if s else wavefunction,
                acc,
            ),
            [SMEM] * 2 + [VMEM] * 4,
            VMEM,
        )
    partial = jnp.swapaxes(acc[:tiles_blk], 0, 1)
    return lax.psum_scatter(partial, ("op", "rep"), scatter_dimension=0, tiled=True)


def shards(wavefunction, left_env, right_env, slot_table):
    op_count = lax.axis_size("op")
    rows = left_env.shape[1] // (2 * op_count)
    fits = lax.axis_size("rep") == 2 and lax.axis_size("blk") == 2
    fits = fits and op_count > 2 and op_count & (op_count - 1) == 0
    fits = fits and rows % 16 == 0 and rows * 2 * op_count == left_env.shape[1]
    form = at_source if fits else gathered
    return form(wavefunction, left_env, right_env, slot_table)


def solution(mesh):
    placed = (
        P(("grp", "blk", "rep"), None, None),
        P(("grp", "op"), None, None),
        P(("grp", "op"), None, None),
        P(None, "op", "blk", None, None, None),
    )
    return jax.shard_map(
        shards,
        mesh=mesh,
        in_specs=placed,
        out_specs=P(("op", "rep"), ("grp", "blk"), None),
        check_vma=False,
    )
```
